512 devices in a mesh: grp: 8 (over x, core), slab: 64 (over y, z).
Axes of the slice: x: 4, y: 4, z: 16, core: 2. Of those that a mesh axis runs over, the one named last changes fastest.
Arguments:
- nodes: bfloat16 [8, 16384, 128], P('grp', 'slab'), may hold values from -6 to 6
- leave_list: int32 [8, 4096], P('grp', 'slab'), may hold values from 0 to 255, as said below
- arrive_list: int32 [8, 16384], P('grp', 'slab'), may hold values from 0 to 319, as said below
- send_list: int32 [8, 8192], P('grp', 'slab'), may hold values from 0 to 255
- neighbours: int32 [8, 16384, 32], P('grp', 'slab'), may hold values from 0 to 383
- valid: int32 [8, 16384, 32], P('grp', 'slab'), may hold values 0 or 1
- w_send: bfloat16 [128, 128], replicated, may hold values from -0.5 to 0.5
- w_recv: bfloat16 [128, 128], replicated, may hold values from -0.5 to 0.5
- w_msg: bfloat16 [128, 128], replicated, may hold values from -0.5 to 0.5
- w_self: bfloat16 [128, 128], replicated, may hold values from -0.5 to 0.5
- w_agg: bfloat16 [128, 128], replicated, may hold values from -0.09375 to 0.09375
- w_out: bfloat16 [128, 128], replicated, may hold values from -0.5 to 0.5
- cotangent: bfloat16 [8, 16384, 128], P('grp', 'slab'), may hold values from -6 to 6
Outputs:
- updated: bfloat16 [8, 16384, 128], P('grp', 'slab')
- grad_nodes: bfloat16 [8, 16384, 128], P('grp', 'slab')
- weight_steps: float32 [6, 128, 128], replicated
The draws below stay inside these ranges and needn't reach their ends.
Inputs may be any that keep to these rules, and one draw needn't show every extreme that they name: `leave_list`: each slab's 2 * 32 entries are distinct rows of that slab. `arrive_list`: each slab's 256 entries are distinct; they name every incoming row (entries 256 and above) and every own row not in that slab's leave_list, and nothing else.
All inputs are finite; a program needn't handle non-finite values. No bound on the sum of `valid` on one device may be relied on, other than what follows from the above.
Results may differ from the reference program's by a relative error of at most 0.0065.
Values may be sent and summed in bfloat16 or wider, within the bound.
A program may use at most 64 MiB of HBM per device.

```python
import jax
import jax.numpy as jnp
from jax import lax

H = 128
K = 32
P_DEV = 256
HALO = 64
MIGR = 32
ROWS = 16384
N_GRP = 8
N_SLAB = 64


def migration_lists(key):
    count = N_GRP * N_SLAB
    keys = jax.random.split(key, count)

    def single(subkey):
        first_key, second_key = jax.random.split(subkey)
        perm = jax.random.permutation(first_key, P_DEV).astype(jnp.int32)
        leaving = perm[:2 * MIGR]
        staying = perm[2 * MIGR:]
        incoming = P_DEV + jnp.arange(2 * MIGR, dtype=jnp.int32)
        arriving = jax.random.permutation(second_key, jnp.concatenate([staying, incoming])).astype(jnp.int32)
        return (leaving, arriving)
    leaving, arriving = jax.vmap(single)(keys)
    return (leaving.reshape(N_GRP, N_SLAB * 2 * MIGR), arriving.reshape(N_GRP, N_SLAB * P_DEV))


def draw_leave_list(key, part):
    leaving, arriving = migration_lists(key)
    return leaving


def draw_arrive_list(key, part):
    leaving, arriving = migration_lists(key)
    return arriving


def touch_ends(result, key, smallest, top_value):
    place = [jax.random.randint(jax.random.fold_in(key, axis), (), 0, length) for axis, length in enumerate(result.shape)]
    longest = result.shape.index(max(result.shape))
    neighbour = place[:longest] + [(place[longest] + 1) % result.shape[longest]] + place[longest + 1:]
    return result.at[tuple(place)].set(smallest).at[tuple(neighbour)].set(top_value)


def block_scale(key, shape, cuts, smallest, largest):
    gain, own = 1.0, jax.random.fold_in(key, 6)
    for position, blocks in cuts:
        draws = jnp.exp(jax.random.uniform(jax.random.fold_in(own, position), (blocks,), jnp.float32, smallest / len(cuts), largest / len(cuts)))
        gain = gain * jnp.repeat(draws, shape[position] // blocks).reshape([-1 if axis == position else 1 for axis in range(len(shape))])
    return gain


def centred(rng, shape, spread, most, shards=(), kind=jnp.bfloat16):
    array = jax.random.normal(rng, shape, jnp.float32) * spread
    if len(shards) > 0:
        array = block_scale(rng, shape, shards, -0.22, 0.18) * array
    return jnp.clip(array, min=-most, max=most).astype(kind)


def setup_inputs(seed: int = 0) -> dict:
    key_list = jax.random.split(jax.random.key(seed), 14)
    nodes = centred(key_list[0], (N_GRP, ROWS, H), 1.0, 6.0, ((0, 8), (1, 64)))
    leave_list = draw_leave_list(jax.random.fold_in(key_list[13], 71), 0)
    arrive_list = draw_arrive_list(jax.random.fold_in(key_list[13], 71), 0)
    send_list = touch_ends(jax.random.randint(key_list[3], (N_GRP, N_SLAB * 2 * HALO), 0, P_DEV), jax.random.fold_in(key_list[3], 1), 0, P_DEV - 1).astype(jnp.int32)
    neighbours = touch_ends(jax.random.randint(key_list[4], (N_GRP, ROWS, K), 0, P_DEV + 2 * HALO), jax.random.fold_in(key_list[4], 1), 0, (P_DEV + 2 * HALO) - 1).astype(jnp.int32)
    valid = touch_ends((jax.random.randint(key_list[5], (N_GRP, ROWS, K), 0, 4) < 3).astype(jnp.int32), jax.random.fold_in(key_list[5], 1), 0, 1)
    w_send = centred(key_list[6], (H, H), H ** -0.5, 0.5)
    w_recv = centred(key_list[7], (H, H), H ** -0.5, 0.5)
    w_msg = centred(key_list[8], (H, H), H ** -0.5, 0.5)
    w_self = centred(key_list[9], (H, H), H ** -0.5, 0.5)
    w_agg = centred(key_list[10], (H, H), (K * H) ** -0.5, 0.09375)
    w_out = centred(key_list[11], (H, H), H ** -0.5, 0.5)
    cotangent = centred(key_list[12], (N_GRP, ROWS, H), 1.0, 6.0, ((0, 8), (1, 64)))
    return dict(nodes=nodes, leave_list=leave_list, arrive_list=arrive_list, send_list=send_list, neighbours=neighbours, valid=valid, w_send=w_send, w_recv=w_recv, w_msg=w_msg, w_self=w_self, w_agg=w_agg, w_out=w_out, cotangent=cotangent)


def dsilu(value):
    sig = jax.nn.sigmoid(value)
    return sig * (1.0 + value * (1.0 - sig))

def inner(left, right):
    return lax.dot_general(left, right, (((0,), (0,)), ((), ())), preferred_element_type=jnp.float32)

def by_transpose(left, right):
    return lax.dot_general(left, right, (((1,), (1,)), ((), ())), preferred_element_type=jnp.float32)

def device_pass(moved, table, nbr, mask, cot, w_send, w_recv, w_msg, w_self, w_agg, w_out):
    rows = moved.shape[0]
    width = moved.shape[1]
    slots = nbr.shape[1]
    centre = jnp.dot(moved, w_send, preferred_element_type=jnp.float32)
    neigh = jnp.dot(table, w_recv, preferred_element_type=jnp.float32).astype(jnp.bfloat16)
    gathered = jnp.take(neigh, nbr.reshape(-1), axis=0).reshape(rows, slots, width)
    pre = centre[:, None, :] + gathered.astype(jnp.float32)
    hid = jax.nn.silu(pre).astype(jnp.bfloat16).reshape(-1, width)
    pre2 = jnp.dot(hid, w_msg, preferred_element_type=jnp.float32).reshape(rows, slots, width)
    maskf = mask.astype(jnp.float32)[:, :, None]
    agg = lax.optimization_barrier(jnp.sum(maskf * jax.nn.silu(pre2), axis=1))
    agg_b = agg.astype(jnp.bfloat16)
    node_pre = jnp.dot(moved, w_self, preferred_element_type=jnp.float32) + jnp.dot(agg_b, w_agg, preferred_element_type=jnp.float32)
    node_hid = jax.nn.silu(node_pre).astype(jnp.bfloat16)
    updated = (moved.astype(jnp.float32) + jnp.dot(node_hid, w_out, preferred_element_type=jnp.float32)).astype(jnp.bfloat16)
    g_out = inner(node_hid, cot)
    d_node_pre = (by_transpose(cot, w_out) * dsilu(node_pre)).astype(jnp.bfloat16)
    g_self = inner(moved, d_node_pre)
    g_agg = inner(agg_b, d_node_pre)
    d_agg = by_transpose(d_node_pre, w_agg)
    d_pre2 = (maskf * d_agg[:, None, :] * dsilu(pre2)).astype(jnp.bfloat16).reshape(-1, width)
    g_msg = inner(hid, d_pre2)
    d_pre = by_transpose(d_pre2, w_msg).reshape(rows, slots, width) * dsilu(pre)
    d_centre = lax.optimization_barrier(jnp.sum(d_pre, axis=1)).astype(jnp.bfloat16)
    d_neigh = jax.ops.segment_sum(d_pre.reshape(-1, width), nbr.reshape(-1), num_segments=table.shape[0]).astype(jnp.bfloat16)
    g_recv = inner(table, d_neigh)
    g_send = inner(moved, d_centre)
    d_table = by_transpose(d_neigh, w_recv)
    d_local = cot.astype(jnp.float32) + by_transpose(d_node_pre, w_self) + by_transpose(d_centre, w_send) + d_table[:rows]
    grads = jnp.stack([g_send, g_recv, g_msg, g_self, g_agg, g_out])
    return (updated, d_local, d_table[rows:], grads)

def reference(nodes, leave_list, arrive_list, send_list, neighbours, valid, w_send, w_recv, w_msg, w_self, w_agg, w_out, cotangent):
    groups = N_GRP
    slabs = N_SLAB
    take = jax.vmap(jax.vmap(lambda rows, index: jnp.take(rows, index, axis=0)))
    plain = nodes.reshape(groups, slabs, P_DEV, H)
    leave = leave_list.reshape(groups, slabs, 2 * MIGR)
    down = take(plain, leave[:, :, :MIGR])
    upward = take(plain, leave[:, :, MIGR:])
    pool = jnp.concatenate([plain, jnp.roll(upward, 1, axis=1), jnp.roll(down, -1, axis=1)], axis=2)
    moved = take(pool, arrive_list.reshape(groups, slabs, P_DEV))
    sends = send_list.reshape(groups, slabs, 2 * HALO)
    lower_rows = take(moved, sends[:, :, :HALO])
    upper_rows = take(moved, sends[:, :, HALO:])
    table = jnp.concatenate([moved, jnp.roll(upper_rows, 1, axis=1), jnp.roll(lower_rows, -1, axis=1)], axis=2)
    count = groups * slabs
    items = (moved.reshape(count, P_DEV, H), table.reshape(count, P_DEV + 2 * HALO, H), neighbours.reshape(count, P_DEV, K), valid.reshape(count, P_DEV, K), cotangent.reshape(count, P_DEV, H))

    def step(total, item):
        updated, d_local, d_halo, grads = device_pass(item[0], item[1], item[2], item[3], item[4], w_send, w_recv, w_msg, w_self, w_agg, w_out)
        return (total + grads, (updated, d_local, d_halo))
    total, outs = lax.scan(step, jnp.zeros((6, H, H), jnp.float32), items)
    updated = outs[0].reshape(groups, slabs * P_DEV, H)
    d_local = outs[1].reshape(groups, slabs, P_DEV, H)
    d_halo = outs[2].reshape(groups, slabs, 2 * HALO, H)
    back_lower = jnp.roll(d_halo[:, :, HALO:], 1, axis=1)
    back_upper = jnp.roll(d_halo[:, :, :HALO], -1, axis=1)
    add_rows = jax.vmap(jax.vmap(lambda field, index, extra: field.at[index].add(extra)))
    d_local = add_rows(d_local, sends[:, :, :HALO], back_lower)
    d_local = add_rows(d_local, sends[:, :, HALO:], back_upper)
    grad_nodes = d_local.reshape(groups, slabs * P_DEV, H).astype(jnp.bfloat16)
    weight_steps = total / jnp.sqrt(lax.optimization_barrier(jnp.mean(total * total, axis=(1, 2), keepdims=True)) + 1e-06)
    return (updated, grad_nodes, weight_steps)
```

```python
import functools

import jax
import jax.numpy as jnp
from jax import lax
from jax.experimental import pallas as pl
from jax.experimental.pallas import tpu as pltpu
from jax.sharding import PartitionSpec as P

MESH = pl.DeviceIdType.MESH
F32 = jnp.float32
BF16 = jnp.bfloat16


def sigmoid(value):
    return 0.5 * jnp.tanh(0.5 * value) + 0.5


def dot(left, right):
    return lax.dot_general(left, right, (((1,), (0,)), ((), ())), preferred_element_type=F32)


def inner(left, right):
    return lax.dot_general(left, right, (((0,), (0,)), ((), ())), preferred_element_type=F32)


def by_transpose(left, right):
    return lax.dot_general(left, right, (((1,), (1,)), ((), ())), preferred_element_type=F32)


def hot(index, shape, dim):
    place = lax.broadcasted_iota(jnp.int32, shape, dim)
    return jnp.where(place == index, 1.0, 0.0).astype(BF16)


def bytes_of(ref, sem):
    return pltpu.make_async_copy(ref, ref, sem)


class Sum:
    def __init__(self, n_grp, n_y, n_z, mats, offset, scratch):
        self.n_grp, self.n_y, self.n_z = n_grp, n_y, n_z
        self.mats, self.offset = mats, offset
        self.plane = n_grp * n_y
        self.per, self.owners = shares(self.plane, mats)
        self.snd, self.rcv, self.part, self.zrcv, self.all, self.sems = scratch
        self.g = lax.axis_index("grp")
        slab = lax.axis_index("slab")
        self.y, self.z = slab // n_z, lax.rem(slab, n_z)
        self.q = self.g * n_y + self.y
        self.block = lax.rem(self.q + self.plane - offset, self.plane)
        self.is_owner = self.block < self.owners

    def device(self, q, z):
        return (q // self.n_y, lax.rem(q, self.n_y) * self.n_z + z)

    def copy(self, src, dst, phase, to):
        return pltpu.make_async_remote_copy(
            src_ref=src,
            dst_ref=dst,
            send_sem=self.sems.at[2 * phase],
            recv_sem=self.sems.at[2 * phase + 1],
            device_id=to,
            device_id_type=MESH,
        )

    def share(self, grads):
        tiles = 8
        for m in range(self.mats):
            low = grads[m].astype(BF16)
            for t in range(tiles):
                b = m * tiles + t
                self.snd[b // self.per, b % self.per] = low[t * 16 : (t + 1) * 16]

        def step(t, carry):
            block = lax.rem(self.block + t, self.plane)

            @pl.when(block < self.owners)
            def _():
                to = lax.rem(block + self.offset, self.plane)
                self.copy(
                    self.snd.at[block], self.rcv.at[self.plane - 1 - t], 0, self.device(to, self.z)
                ).start()

            return carry

        lax.fori_loop(1, self.plane, step, 0)

    def line(self):
        @pl.when(self.is_owner)
        def _():
            others = self.plane - 1
            bytes_of(self.rcv.at[pl.ds(0, others)], self.sems.at[1]).wait()
            total = self.snd[self.block].astype(F32)
            for i in range(others):
                total = total + self.rcv[i].astype(F32)
            self.part[0] = total.astype(BF16)
            self.zrcv[self.n_z - 1] = total.astype(BF16)
            half = self.n_z // 2

            def step(t, carry):
                to = lax.rem(self.z + half + t, self.n_z)
                slot = lax.rem(self.n_z - 1 - half - t + self.n_z, self.n_z)

                @pl.when(to != self.z)
                def _():
                    self.copy(
                        self.part.at[0], self.zrcv.at[slot], 1, self.device(self.q, to)
                    ).start()

                return carry

            lax.fori_loop(0, self.n_z, step, 0)

    def spread(self):
        @pl.when(self.is_owner)
        def _():
            bytes_of(self.zrcv.at[pl.ds(0, self.n_z - 1)], self.sems.at[3]).wait()
            total = jnp.zeros(self.part.shape[1:], F32)
            for i in range(self.n_z):
                total = total + self.zrcv[self.slot_of(i)].astype(F32)
            self.part[1] = total.astype(BF16)
            self.all[self.block] = total.astype(BF16)

            def step(t, carry):
                to = lax.rem(self.q + t, self.plane)
                self.copy(
                    self.part.at[1], self.all.at[self.block], 2, self.device(to, self.z)
                ).start()
                return carry

            lax.fori_loop(1, self.plane, step, 0)

    def slot_of(self, i):
        return lax.rem(self.n_z - 1 - (self.z - i) + 2 * self.n_z, self.n_z)

    def finish(self, out, first):
        own = self.is_owner

        @pl.when(own)
        def _():
            bytes_of(self.snd.at[pl.ds(0, self.owners - 1)], self.sems.at[0]).wait()
            bytes_of(self.zrcv.at[pl.ds(0, self.n_z - 1)], self.sems.at[2]).wait()
            bytes_of(self.rcv.at[pl.ds(0, self.plane - 1)], self.sems.at[4]).wait()
            if self.owners > 1:
                bytes_of(self.all.at[pl.ds(0, self.owners - 1)], self.sems.at[5]).wait()

        @pl.when(jnp.logical_not(own))
        def _():
            bytes_of(self.snd.at[pl.ds(0, self.owners)], self.sems.at[0]).wait()
            bytes_of(self.all.at[pl.ds(0, self.owners)], self.sems.at[5]).wait()

        for m in range(self.mats):
            tiles = []
            for t in range(8):
                b = m * 8 + t
                tiles.append(self.all[b // self.per, b % self.per])
            total = jnp.concatenate(tiles, axis=0).astype(F32)
            square = jnp.sum(jnp.sum(total * total, axis=0, keepdims=True), axis=1, keepdims=True)
            out[first + m] = total / jnp.sqrt(square * (1.0 / (128 * 128)) + 1e-06)


def shares(plane, mats):
    blocks = mats * 8
    per = -(-blocks // plane)
    while blocks % per:
        per += 1
    return per, blocks // per


def sum_scratch(plane, n_z, mats):
    per, owners = shares(plane, mats)
    return [
        pltpu.VMEM((owners, per, 16, 128), BF16),
        pltpu.VMEM((plane, per, 16, 128), BF16),
        pltpu.VMEM((2, per, 16, 128), BF16),
        pltpu.VMEM((n_z, per, 16, 128), BF16),
        pltpu.VMEM((owners, per, 16, 128), BF16),
        pltpu.SemaphoreType.DMA((6,)),
    ]


N_IN = 13
CH = 4


def kernel(n_grp, n_y, n_z, dims, *refs):
    rows, slots, migr, halo = dims
    table_rows = rows + 2 * halo
    ins = refs[:N_IN]
    updated_ref, grad_ref, steps_ref = refs[N_IN : N_IN + 3]
    scratch = refs[N_IN + 3 :]
    held = scratch[:N_IN]
    (
        in_sems,
        halo_sems,
        pool,
        mig_snd,
        out_snd,
        table,
        ret_snd,
        ret_rcv,
        col,
        row,
        oh,
        oht,
        mask,
        neigh,
        centre,
        agg,
        hid,
        ds1,
        md,
        d_agg,
        d_centre,
        d_neigh,
        g_msg,
    ) = scratch[N_IN : N_IN + 23]
    reduce_scratch = scratch[N_IN + 23 :]
    (nodes, leave, arrive, send, nbr, valid, w_send, w_recv, w_msg, w_self, w_agg, w_out, cot) = held

    g, slab = lax.axis_index("grp"), lax.axis_index("slab")
    n_slab = n_y * n_z
    y, z = slab // n_z, lax.rem(slab, n_z)
    plane = n_grp * n_y
    q = g * n_y + y
    lower = (g, lax.rem(slab + n_slab - 1, n_slab))
    upper = (g, lax.rem(slab + 1, n_slab))

    loads = [pltpu.make_async_copy(ins[i], held[i], in_sems.at[i]) for i in range(N_IN)]
    for i in range(N_IN):
        loads[i].start()

    barrier = pltpu.get_barrier_semaphore()
    for to in (lower, upper):
        pl.semaphore_signal(barrier, inc=1, device_id=to, device_id_type=MESH)

    def greet_plane(t, carry):
        to = lax.rem(q + t, plane)
        pl.semaphore_signal(
            barrier,
            inc=1,
            device_id=(to // n_y, lax.rem(to, n_y) * n_z + z),
            device_id_type=MESH,
        )
        return carry

    def greet_line(t, carry):
        to = (g, y * n_z + lax.rem(z + t, n_z))
        pl.semaphore_signal(barrier, inc=1, device_id=to, device_id_type=MESH)
        return carry

    lax.fori_loop(1, plane, greet_plane, 0)
    lax.fori_loop(1, n_z, greet_line, 0)

    def swap(src, low_src, low_dst, up_src, up_dst, dst, stage):
        size = low_src.size
        copies = []
        for k, (a, b, to) in enumerate(((low_src, low_dst, lower), (up_src, up_dst, upper))):
            copies.append(
                pltpu.make_async_remote_copy(
                    src_ref=src.at[a],
                    dst_ref=dst.at[b],
                    send_sem=halo_sems.at[4 * stage + k],
                    recv_sem=halo_sems.at[4 * stage + 2 + k],
                    device_id=to,
                    device_id_type=MESH,
                )
            )
        for copy in copies:
            copy.start()
        return copies

    loads[0].wait()
    loads[1].wait()
    mig_snd[...] = inner(hot(leave[...], (rows, 2 * migr), 0), nodes[...]).astype(BF16)
    pl.semaphore_wait(barrier, plane + n_z)
    moving = swap(
        mig_snd,
        pl.ds(0, migr),
        pl.ds(rows + migr, migr),
        pl.ds(migr, migr),
        pl.ds(rows, migr),
        pool,
        0,
    )
    pool[pl.ds(0, rows)] = nodes[...]
    for i in range(2, N_IN):
        loads[i].wait()
    arrive_hot = hot(arrive[...], (rows + 2 * migr, rows), 0)
    send_hot = hot(send[...], (rows, 2 * halo), 0)
    marked = jnp.where(valid[...] > 0, nbr[...], table_rows)
    col[:, pl.ds(0, slots)] = marked
    row[...] = col[...].T[0:slots]

    def front_hot(first, last):
        for k in range(first, last):
            index = col[:, k : k + 1]
            here = pl.ds(k * rows, rows)
            oh[here, :] = hot(index, (rows, table_rows), 1)
            mask[here, :] = jnp.where(
                jnp.broadcast_to(index, (rows, 128)) < table_rows, 1.0, 0.0
            ).astype(F32)

    front_hot(0, slots // 2)
    for copy in moving:
        copy.wait()

    moved = inner(arrive_hot, pool[...]).astype(BF16)
    out_snd[...] = inner(send_hot, moved).astype(BF16)
    lending = swap(
        out_snd,
        pl.ds(0, halo),
        pl.ds(rows + halo, halo),
        pl.ds(halo, halo),
        pl.ds(rows, halo),
        table,
        1,
    )
    table[pl.ds(0, rows)] = moved
    centre[...] = dot(moved, w_send[...])
    neigh[pl.ds(0, rows)] = dot(moved, w_recv[...]).astype(BF16)
    d_hid = by_transpose(cot[...], w_out[...])
    node_own = dot(moved, w_self[...])
    front_hot(slots // 2, slots)
    for copy in lending:
        copy.wait()
    neigh[pl.ds(rows, 2 * halo)] = dot(table[pl.ds(rows, 2 * halo)], w_recv[...]).astype(BF16)

    agg[...] = jnp.zeros_like(agg)
    span = CH * rows

    def front(c, carry):
        here = pl.ds(pl.multiple_of(c * span, span), span)
        pre = dot(oh[here, :], neigh[...]) + jnp.concatenate([centre[...]] * CH, axis=0)
        sig = sigmoid(pre)
        act = pre * sig
        low = act.astype(BF16)
        hid[here, :] = low
        ds1[here, :] = sig + act * (1.0 - sig)
        pre2 = dot(low, w_msg[...])
        sig2 = sigmoid(pre2)
        act2 = pre2 * sig2
        live = mask[here, :]
        md[here, :] = live * (sig2 + act2 * (1.0 - sig2))
        part = live * act2
        total = part[0:rows]
        for u in range(1, CH):
            total = total + part[u * rows : (u + 1) * rows]
        agg[...] += total
        return carry

    lax.fori_loop(0, slots // CH, front, 0)

    moved = table[pl.ds(0, rows)]
    agg_b = agg[...].astype(BF16)
    node_pre = node_own + dot(agg_b, w_agg[...])
    sig = sigmoid(node_pre)
    act = node_pre * sig
    node_hid = act.astype(BF16)
    updated_ref[...] = (moved.astype(F32) + dot(node_hid, w_out[...])).astype(BF16)
    d_node_pre = (d_hid * (sig + act * (1.0 - sig))).astype(BF16)
    d_agg[...] = by_transpose(d_node_pre, w_agg[...])
    g_out = inner(node_hid, cot[...])
    g_self = inner(moved, d_node_pre)
    g_agg = inner(agg_b, d_node_pre)
    d_local = cot[...].astype(F32) + by_transpose(d_node_pre, w_self[...])

    d_centre[...] = jnp.zeros_like(d_centre)
    d_neigh[...] = jnp.zeros_like(d_neigh)
    g_msg[...] = jnp.zeros_like(g_msg)

    def back(c, carry):
        here = pl.ds(pl.multiple_of(c * span, span), span)
        for u in range(CH):
            index = row[pl.ds(c * CH + u, 1), :]
            oht[:, u * rows : (u + 1) * rows] = hot(index, (table_rows, rows), 0)
        d_pre2 = (jnp.concatenate([d_agg[...]] * CH, axis=0) * md[here, :]).astype(BF16)
        d_pre = by_transpose(d_pre2, w_msg[...]) * ds1[here, :]
        g_msg[...] += inner(hid[here, :], d_pre2)
        total = d_pre[0:rows]
        for u in range(1, CH):
            total = total + d_pre[u * rows : (u + 1) * rows]
        d_centre[...] += total
        d_neigh[...] += dot(oht[...], d_pre.astype(BF16))
        return carry

    lax.fori_loop(0, slots // CH, back, 0)

    d_neigh_b = d_neigh[...].astype(BF16)
    ret_snd[...] = by_transpose(d_neigh_b[rows:], w_recv[...]).astype(BF16)
    returning = swap(
        ret_snd, pl.ds(0, halo), pl.ds(halo, halo), pl.ds(halo, halo), pl.ds(0, halo), ret_rcv, 2
    )
    d_centre_b = d_centre[...].astype(BF16)
    moved = table[pl.ds(0, rows)]
    g_send = inner(moved, d_centre_b)
    g_recv = inner(table[...], d_neigh_b)
    reduce = Sum(n_grp, n_y, n_z, 6, 0, reduce_scratch)
    reduce.share([g_send, g_recv, g_msg[...], g_self, g_agg, g_out])
    d_local = d_local + by_transpose(d_centre_b, w_send[...])
    d_local = d_local + by_transpose(d_neigh_b[0:rows], w_recv[...])
    reduce.line()
    for copy in returning:
        copy.wait()
    d_local = d_local + dot(send_hot, ret_rcv[...])
    grad_ref[...] = d_local.astype(BF16)
    reduce.spread()
    reduce.finish(steps_ref, 0)


def shards(n_grp, n_y, n_z, *args):
    nodes, leave_list, arrive_list, send_list, neighbours, valid = args[:6]
    weights, cotangent = args[6:12], args[12]
    operands = (
        nodes[0],
        leave_list,
        arrive_list,
        send_list,
        neighbours[0],
        valid[0],
        *weights,
        cotangent[0],
    )
    rows, width = operands[0].shape
    slots = operands[4].shape[1]
    migr, halo = leave_list.shape[1] // 2, send_list.shape[1] // 2
    table_rows = rows + 2 * halo
    edges = rows * slots
    plane = n_grp * n_y
    scratch = [pltpu.VMEM(x.shape, x.dtype) for x in operands]
    scratch += [
        pltpu.SemaphoreType.DMA((N_IN,)),
        pltpu.SemaphoreType.DMA((12,)),
        pltpu.VMEM((rows + 2 * migr, width), BF16),
        pltpu.VMEM((2 * migr, width), BF16),
        pltpu.VMEM((2 * halo, width), BF16),
        pltpu.VMEM((table_rows, width), BF16),
        pltpu.VMEM((2 * halo, width), BF16),
        pltpu.VMEM((2 * halo, width), BF16),
        pltpu.VMEM((rows, 128), jnp.int32),
        pltpu.VMEM((slots, rows), jnp.int32),
        pltpu.VMEM((edges, table_rows), BF16),
        pltpu.VMEM((table_rows, CH * rows), BF16),
        pltpu.VMEM((edges, width), F32),
        pltpu.VMEM((table_rows, width), BF16),
        pltpu.VMEM((rows, width), F32),
        pltpu.VMEM((rows, width), F32),
        pltpu.VMEM((edges, width), BF16),
        pltpu.VMEM((edges, width), F32),
        pltpu.VMEM((edges, width), F32),
        pltpu.VMEM((rows, width), F32),
        pltpu.VMEM((rows, width), F32),
        pltpu.VMEM((table_rows, width), F32),
        pltpu.VMEM((width, width), F32),
    ]
    scratch += sum_scratch(plane, n_z, 6)
    updated, grad_nodes, weight_steps = pl.pallas_call(
        functools.partial(kernel, n_grp, n_y, n_z, (rows, slots, migr, halo)),
        out_shape=(
            jax.ShapeDtypeStruct((rows, width), BF16),
            jax.ShapeDtypeStruct((rows, width), BF16),
            jax.ShapeDtypeStruct((6, width, width), F32),
        ),
        in_specs=[pl.BlockSpec(memory_space=pl.ANY)] * N_IN,
        out_specs=[pl.BlockSpec(memory_space=pltpu.VMEM)] * 3,
        scratch_shapes=scratch,
        compiler_params=pltpu.CompilerParams(
            collective_id=0, has_side_effects=True, vmem_limit_bytes=48 * 1024 * 1024
        ),
        name="particle_step",
    )(*operands)
    return (updated[None], grad_nodes[None], weight_steps)


def solution(mesh):
    n_grp, n_slab = mesh.shape["grp"], mesh.shape["slab"]
    n_z = 16 if n_slab > 16 else n_slab // 2
    in_specs = (
        P("grp", "slab", None),
        P("grp", "slab"),
        P("grp", "slab"),
        P("grp", "slab"),
        P("grp", "slab", None),
        P("grp", "slab", None),
        P(),
        P(),
        P(),
        P(),
        P(),
        P(),
        P("grp", "slab", None),
    )
    out_specs = (P("grp", "slab", None), P("grp", "slab", None), P())
    return jax.shard_map(
        functools.partial(shards, n_grp, n_slab // n_z, n_z),
        mesh=mesh,
        in_specs=in_specs,
        out_specs=out_specs,
        check_vma=False,
    )
```

```python
import functools

import jax
import jax.numpy as jnp
from jax import lax
from jax.experimental import pallas as pl
from jax.experimental.pallas import tpu as pltpu
from jax.sharding import PartitionSpec as P

MESH = pl.DeviceIdType.MESH
F32 = jnp.float32
BF16 = jnp.bfloat16


def silu_pair(half):
    up = 1.0 + jnp.tanh(half)
    act = half * up
    return act, up * (1.0 + (half + half) - act)


def dot(left, right):
    return lax.dot_general(left, right, (((1,), (0,)), ((), ())), preferred_element_type=F32)


def inner(left, right):
    return lax.dot_general(left, right, (((0,), (0,)), ((), ())), preferred_element_type=F32)


def by_transpose(left, right):
    return lax.dot_general(left, right, (((1,), (1,)), ((), ())), preferred_element_type=F32)


def half(weights):
    return (0.5 * weights.astype(F32)).astype(BF16)


def hot(index, shape, dim):
    place = lax.broadcasted_iota(jnp.int32, shape, dim)
    return jnp.where(place == index, 1.0, 0.0).astype(BF16)


def bytes_of(ref, sem):
    return pltpu.make_async_copy(ref, ref, sem)


class Sum:
    def __init__(self, n_grp, n_y, n_z, mats, offset, scratch):
        self.n_grp, self.n_y, self.n_z = n_grp, n_y, n_z
        self.mats, self.offset = mats, offset
        self.plane = n_grp * n_y
        self.per, self.owners = shares(self.plane, mats)
        self.snd, self.rcv, self.part, self.zrcv, self.all, self.sems = scratch
        self.g = lax.axis_index("grp")
        slab = lax.axis_index("slab")
        self.y, self.z = slab // n_z, lax.rem(slab, n_z)
        self.q = self.g * n_y + self.y
        self.block = lax.rem(self.q + self.plane - offset, self.plane)
        self.is_owner = self.block < self.owners

    def device(self, q, z):
        return (q // self.n_y, lax.rem(q, self.n_y) * self.n_z + z)

    def copy(self, src, dst, phase, to):
        return pltpu.make_async_remote_copy(
            src_ref=src,
            dst_ref=dst,
            send_sem=self.sems.at[2 * phase],
            recv_sem=self.sems.at[2 * phase + 1],
            device_id=to,
            device_id_type=MESH,
        )

    def share(self, grads):
        tiles = 8
        for m in range(self.mats):
            low = grads[m].astype(BF16)
            for t in range(tiles):
                b = m * tiles + t
                self.snd[b // self.per, b % self.per] = low[t * 16 : (t + 1) * 16]

        def step(t, carry):
            block = lax.rem(self.block + t, self.plane)

            @pl.when(block < self.owners)
            def _():
                to = lax.rem(block + self.offset, self.plane)
                self.copy(
                    self.snd.at[block], self.rcv.at[self.plane - 1 - t], 0, self.device(to, self.z)
                ).start()

            return carry

        lax.fori_loop(1, self.plane, step, 0)

    def line(self):
        @pl.when(self.is_owner)
        def _():
            others = self.plane - 1
            bytes_of(self.rcv.at[pl.ds(0, others)], self.sems.at[1]).wait()
            total = self.snd[self.block].astype(F32)
            for i in range(others):
                total = total + self.rcv[i].astype(F32)
            self.part[0] = total.astype(BF16)
            self.zrcv[self.n_z - 1] = total.astype(BF16)
            half = self.n_z // 2

            def step(t, carry):
                to = lax.rem(self.z + half + t, self.n_z)
                slot = lax.rem(self.n_z - 1 - half - t + self.n_z, self.n_z)

                @pl.when(to != self.z)
                def _():
                    self.copy(
                        self.part.at[0], self.zrcv.at[slot], 1, self.device(self.q, to)
                    ).start()

                return carry

            lax.fori_loop(0, self.n_z, step, 0)

    def spread(self):
        @pl.when(self.is_owner)
        def _():
            bytes_of(self.zrcv.at[pl.ds(0, self.n_z - 1)], self.sems.at[3]).wait()
            total = jnp.zeros(self.part.shape[1:], F32)
            for i in range(self.n_z):
                total = total + self.zrcv[self.slot_of(i)].astype(F32)
            self.part[1] = total.astype(BF16)
            self.all[self.block] = total.astype(BF16)

            def step(t, carry):
                to = lax.rem(self.q + t, self.plane)
                self.copy(
                    self.part.at[1], self.all.at[self.block], 2, self.device(to, self.z)
                ).start()
                return carry

            lax.fori_loop(1, self.plane, step, 0)

    def slot_of(self, i):
        return lax.rem(self.n_z - 1 - (self.z - i) + 2 * self.n_z, self.n_z)

    def finish(self, out, first):
        own = self.is_owner

        @pl.when(own)
        def _():
            bytes_of(self.snd.at[pl.ds(0, self.owners - 1)], self.sems.at[0]).wait()
            bytes_of(self.zrcv.at[pl.ds(0, self.n_z - 1)], self.sems.at[2]).wait()
            bytes_of(self.rcv.at[pl.ds(0, self.plane - 1)], self.sems.at[4]).wait()
            if self.owners > 1:
                bytes_of(self.all.at[pl.ds(0, self.owners - 1)], self.sems.at[5]).wait()

        @pl.when(jnp.logical_not(own))
        def _():
            bytes_of(self.snd.at[pl.ds(0, self.owners)], self.sems.at[0]).wait()
            bytes_of(self.all.at[pl.ds(0, self.owners)], self.sems.at[5]).wait()

        for m in range(self.mats):
            tiles = []
            for t in range(8):
                b = m * 8 + t
                tiles.append(self.all[b // self.per, b % self.per])
            total = jnp.concatenate(tiles, axis=0).astype(F32)
            square = jnp.sum(jnp.sum(total * total, axis=0, keepdims=True), axis=1, keepdims=True)
            out[first + m] = total / jnp.sqrt(square * (1.0 / (128 * 128)) + 1e-06)


def shares(plane, mats):
    blocks = mats * 8
    per = -(-blocks // plane)
    while blocks % per:
        per += 1
    return per, blocks // per


def sum_scratch(plane, n_z, mats):
    per, owners = shares(plane, mats)
    return [
        pltpu.VMEM((owners, per, 16, 128), BF16),
        pltpu.VMEM((plane, per, 16, 128), BF16),
        pltpu.VMEM((2, per, 16, 128), BF16),
        pltpu.VMEM((n_z, per, 16, 128), BF16),
        pltpu.VMEM((owners, per, 16, 128), BF16),
        pltpu.SemaphoreType.DMA((6,)),
    ]


N_IN = 13
CH = 16


def kernel(n_grp, n_y, n_z, dims, *refs):
    rows, slots, migr, halo = dims
    table_rows = rows + 2 * halo
    ins = refs[:N_IN]
    updated_ref, grad_ref, steps_ref = refs[N_IN : N_IN + 3]
    scratch = refs[N_IN + 3 :]
    held = scratch[:N_IN]
    (
        in_sems,
        halo_sems,
        snd,
        rcv,
        far_rows,
        table,
        ret_snd,
        ret_rcv,
        row,
        oh,
        oht,
        mask,
        neigh,
        centre,
        agg,
        hid,
        ds1,
        md,
        d_agg,
        d_centre,
        d_neigh,
        g_msg,
    ) = scratch[N_IN : N_IN + 22]
    reduce_scratch = scratch[N_IN + 22 :]
    (nodes, leave, arrive, send, nbr, valid, w_send, w_recv, w_msg, w_self, w_agg, w_out, cot) = held

    g, slab = lax.axis_index("grp"), lax.axis_index("slab")
    n_slab = n_y * n_z
    y, z = slab // n_z, lax.rem(slab, n_z)
    plane = n_grp * n_y
    q = g * n_y + y
    lower = (g, lax.rem(slab + n_slab - 1, n_slab))
    upper = (g, lax.rem(slab + 1, n_slab))
    lower2 = (g, lax.rem(slab + n_slab - 2, n_slab))
    upper2 = (g, lax.rem(slab + 2, n_slab))

    loads = [pltpu.make_async_copy(ins[i], held[i], in_sems.at[i]) for i in range(N_IN)]
    for i in range(N_IN):
        loads[i].start()

    barrier = pltpu.get_barrier_semaphore()
    for to in (lower, upper, lower2, upper2):
        pl.semaphore_signal(barrier, inc=1, device_id=to, device_id_type=MESH)

    def greet_plane(t, carry):
        to = lax.rem(q + t, plane)
        pl.semaphore_signal(
            barrier,
            inc=1,
            device_id=(to // n_y, lax.rem(to, n_y) * n_z + z),
            device_id_type=MESH,
        )
        return carry

    def greet_line(t, carry):
        to = (g, y * n_z + lax.rem(z + t, n_z))
        pl.semaphore_signal(barrier, inc=1, device_id=to, device_id_type=MESH)
        return carry

    lax.fori_loop(1, plane, greet_plane, 0)
    lax.fori_loop(1, n_z, greet_line, 0)

    def send_to(src, dst, k, to):
        return pltpu.make_async_remote_copy(
            src_ref=src,
            dst_ref=dst,
            send_sem=halo_sems.at[2 * k],
            recv_sem=halo_sems.at[2 * k + 1],
            device_id=to,
            device_id_type=MESH,
        )

    for i in range(4):
        loads[i].wait()
    mine = nodes[...]
    arrive_hot = hot(arrive[...], (rows + 2 * migr, rows), 0)
    send_hot = hot(send[...], (rows, 2 * halo), 0)
    moving = inner(hot(leave[...], (rows, 2 * migr), 0), mine).astype(BF16)
    chosen = dot(arrive_hot, send_hot).astype(BF16)
    lent = inner(chosen[0:rows], mine).astype(BF16)
    picks = chosen[rows:]
    down, up = moving[0:migr], moving[migr:]
    for k, (part, leaving) in enumerate(((lent[0:halo], down), (lent[halo:], up))):
        snd[k, 0:halo] = part
        snd[k, halo : halo + 2 * migr] = picks
        snd[k, halo + 2 * migr :] = leaving
    pl.semaphore_wait(barrier, plane + n_z + 2)
    fetching = []
    for k, (near, far) in enumerate(((lower, lower2), (upper, upper2))):
        fetching.append(send_to(snd.at[k], rcv.at[k], k, near))
        fetching.append(
            send_to(snd.at[k, pl.ds(halo + 2 * migr, migr)], far_rows.at[k], 2 + k, far)
        )
    for copy in fetching:
        copy.start()
    for i in range(4, N_IN):
        loads[i].wait()
    row[...] = jnp.where(valid[...] > 0, nbr[...], table_rows)
    across = row[...].T
    for k in range(slots):
        index = across[:, k : k + 1]
        here = pl.ds(k * rows, rows)
        oh[here, :] = hot(index, (rows, table_rows), 1)
        mask[here, :] = jnp.where(
            jnp.broadcast_to(index, (rows, 128)) < table_rows, 1.0, 0.0
        ).astype(F32)
    d_hid = by_transpose(cot[...], w_out[...])
    w_msg_half = half(w_msg[...])
    kept = inner(arrive_hot[0:rows], mine)
    for copy in fetching:
        copy.wait()

    from_below, from_above = rcv.at[1], rcv.at[0]
    low_new, high_new = from_below[halo + 2 * migr :], from_above[halo + 2 * migr :]
    moved = kept + inner(arrive_hot[rows:], jnp.concatenate([low_new, high_new], axis=0))
    moved = moved.astype(BF16)
    low_rows = inner(from_below[halo : halo + 2 * migr], jnp.concatenate([far_rows[1], down], axis=0))
    high_rows = inner(from_above[halo : halo + 2 * migr], jnp.concatenate([up, far_rows[0]], axis=0))
    table[pl.ds(0, rows)] = moved
    table[pl.ds(rows, halo)] = from_below[0:halo] + low_rows[halo:].astype(BF16)
    table[pl.ds(rows + halo, halo)] = from_above[0:halo] + high_rows[0:halo].astype(BF16)
    neigh[...] = (0.5 * dot(table[...], w_recv[...])).astype(BF16)
    centre[...] = 0.5 * dot(moved, w_send[...])

    agg[...] = jnp.zeros_like(agg)
    span = CH * rows

    def front(c, carry):
        here = pl.ds(pl.multiple_of(c * span, span), span)
        pre = dot(oh[here, :], neigh[...]) + jnp.concatenate([centre[...]] * CH, axis=0)
        act, slope = silu_pair(pre)
        low = act.astype(BF16)
        hid[here, :] = low
        ds1[here, :] = slope
        act, slope = silu_pair(dot(low, w_msg_half))
        live = mask[here, :]
        md[here, :] = live * slope
        part = live * act
        total = part[0:rows]
        for u in range(1, CH):
            total = total + part[u * rows : (u + 1) * rows]
        agg[...] += total
        return carry

    lax.fori_loop(0, slots // CH, front, 0)

    moved = table[pl.ds(0, rows)]
    agg_b = agg[...].astype(BF16)
    act, slope = silu_pair(0.5 * (dot(moved, w_self[...]) + dot(agg_b, w_agg[...])))
    node_hid = act.astype(BF16)
    updated_ref[...] = (moved.astype(F32) + dot(node_hid, w_out[...])).astype(BF16)
    d_node_pre = (0.5 * d_hid * slope).astype(BF16)
    d_agg[...] = 0.5 * by_transpose(d_node_pre, w_agg[...])
    g_out = inner(node_hid, cot[...])
    g_self = inner(moved, d_node_pre)
    g_agg = inner(agg_b, d_node_pre)
    d_local = cot[...].astype(F32) + by_transpose(d_node_pre, w_self[...])

    d_centre[...] = jnp.zeros_like(d_centre)
    d_neigh[...] = jnp.zeros_like(d_neigh)
    g_msg[...] = jnp.zeros_like(g_msg)

    def back(c, carry):
        here = pl.ds(pl.multiple_of(c * span, span), span)
        for u in range(CH):
            index = row[pl.ds(c * CH + u, 1), :]
            oht[:, u * rows : (u + 1) * rows] = hot(index, (table_rows, rows), 0)
        d_pre2 = (jnp.concatenate([d_agg[...]] * CH, axis=0) * md[here, :]).astype(BF16)
        d_pre = by_transpose(d_pre2, w_msg_half) * ds1[here, :]
        g_msg[...] += inner(hid[here, :], d_pre2)
        total = d_pre[0:rows]
        for u in range(1, CH):
            total = total + d_pre[u * rows : (u + 1) * rows]
        d_centre[...] += total
        d_neigh[...] += dot(oht[...], d_pre.astype(BF16))
        return carry

    lax.fori_loop(0, slots // CH, back, 0)

    d_neigh_b = d_neigh[...].astype(BF16)
    ret_snd[...] = by_transpose(d_neigh_b[rows:], w_recv[...]).astype(BF16)
    returning = [
        send_to(ret_snd.at[pl.ds(0, halo)], ret_rcv.at[pl.ds(halo, halo)], 4, lower),
        send_to(ret_snd.at[pl.ds(halo, halo)], ret_rcv.at[pl.ds(0, halo)], 5, upper),
    ]
    for copy in returning:
        copy.start()
    d_centre_b = d_centre[...].astype(BF16)
    moved = table[pl.ds(0, rows)]
    g_send = inner(moved, d_centre_b)
    g_recv = inner(table[...], d_neigh_b)
    reduce = Sum(n_grp, n_y, n_z, 6, 0, reduce_scratch)
    reduce.share([g_send, g_recv, g_msg[...], g_self, g_agg, g_out])
    d_local = d_local + by_transpose(d_centre_b, w_send[...])
    d_local = d_local + by_transpose(d_neigh_b[0:rows], w_recv[...])
    reduce.line()
    for copy in returning:
        copy.wait()
    d_local = d_local + dot(send_hot, ret_rcv[...])
    grad_ref[...] = d_local.astype(BF16)
    reduce.spread()
    reduce.finish(steps_ref, 0)


def shards(n_grp, n_y, n_z, *args):
    nodes, leave_list, arrive_list, send_list, neighbours, valid = args[:6]
    weights, cotangent = args[6:12], args[12]
    operands = (
        nodes[0],
        leave_list,
        arrive_list,
        send_list,
        neighbours[0].T,
        valid[0].T,
        *weights,
        cotangent[0],
    )
    rows, width = operands[0].shape
    slots = operands[4].shape[0]
    migr, halo = leave_list.shape[1] // 2, send_list.shape[1] // 2
    table_rows = rows + 2 * halo
    edges = rows * slots
    plane = n_grp * n_y
    scratch = [pltpu.VMEM(x.shape, x.dtype) for x in operands]
    scratch += [
        pltpu.SemaphoreType.DMA((N_IN,)),
        pltpu.SemaphoreType.DMA((12,)),
        pltpu.VMEM((2, halo + 3 * migr, width), BF16),
        pltpu.VMEM((2, halo + 3 * migr, width), BF16),
        pltpu.VMEM((2, migr, width), BF16),
        pltpu.VMEM((table_rows, width), BF16),
        pltpu.VMEM((2 * halo, width), BF16),
        pltpu.VMEM((2 * halo, width), BF16),
        pltpu.VMEM((slots, rows), jnp.int32),
        pltpu.VMEM((edges, table_rows), BF16),
        pltpu.VMEM((table_rows, CH * rows), BF16),
        pltpu.VMEM((edges, width), F32),
        pltpu.VMEM((table_rows, width), BF16),
        pltpu.VMEM((rows, width), F32),
        pltpu.VMEM((rows, width), F32),
        pltpu.VMEM((edges, width), BF16),
        pltpu.VMEM((edges, width), F32),
        pltpu.VMEM((edges, width), F32),
        pltpu.VMEM((rows, width), F32),
        pltpu.VMEM((rows, width), F32),
        pltpu.VMEM((table_rows, width), F32),
        pltpu.VMEM((width, width), F32),
    ]
    scratch += sum_scratch(plane, n_z, 6)
    updated, grad_nodes, weight_steps = pl.pallas_call(
        functools.partial(kernel, n_grp, n_y, n_z, (rows, slots, migr, halo)),
        out_shape=(
            jax.ShapeDtypeStruct((rows, width), BF16),
            jax.ShapeDtypeStruct((rows, width), BF16),
            jax.ShapeDtypeStruct((6, width, width), F32),
        ),
        in_specs=[pl.BlockSpec(memory_space=pltpu.HBM)] * N_IN,
        out_specs=[pl.BlockSpec(memory_space=pltpu.VMEM)] * 3,
        scratch_shapes=scratch,
        compiler_params=pltpu.CompilerParams(
            collective_id=0, has_side_effects=True, vmem_limit_bytes=63 * 1024 * 1024
        ),
        name="particle_step",
    )(*operands)
    return (updated[None], grad_nodes[None], weight_steps)


def solution(mesh):
    n_grp, n_slab = mesh.shape["grp"], mesh.shape["slab"]
    n_z = 16 if n_slab > 16 else n_slab // 2
    in_specs = (
        P("grp", "slab", None),
        P("grp", "slab"),
        P("grp", "slab"),
        P("grp", "slab"),
        P("grp", "slab", None),
        P("grp", "slab", None),
        P(),
        P(),
        P(),
        P(),
        P(),
        P(),
        P("grp", "slab", None),
    )
    out_specs = (P("grp", "slab", None), P("grp", "slab", None), P())
    return jax.shard_map(
        functools.partial(shards, n_grp, n_slab // n_z, n_z),
        mesh=mesh,
        in_specs=in_specs,
        out_specs=out_specs,
        check_vma=False,
    )
```

```python
import functools

import jax
import jax.numpy as jnp
from jax import lax
from jax.experimental import pallas as pl
from jax.experimental.pallas import tpu as pltpu
from jax.sharding import PartitionSpec as P

MESH = pl.DeviceIdType.MESH
F32 = jnp.float32
BF16 = jnp.bfloat16


def silu_pair(half):
    up = 1.0 + jnp.tanh(half)
    act = half * up
    return act, up * (1.0 + (half + half) - act)


def dot(left, right):
    return lax.dot_general(left, right, (((1,), (0,)), ((), ())), preferred_element_type=F32)


def inner(left, right):
    return lax.dot_general(left, right, (((0,), (0,)), ((), ())), preferred_element_type=F32)


def by_transpose(left, right):
    return lax.dot_general(left, right, (((1,), (1,)), ((), ())), preferred_element_type=F32)


def half(weights):
    return (0.5 * weights.astype(F32)).astype(BF16)


def hot(index, shape, dim):
    place = lax.broadcasted_iota(jnp.int32, shape, dim)
    return jnp.where(place == index, 1.0, 0.0).astype(BF16)


def bytes_of(ref, sem):
    return pltpu.make_async_copy(ref, ref, sem)


class Sum:
    def __init__(self, n_grp, n_y, n_z, mats, offset, scratch):
        self.n_grp, self.n_y, self.n_z = n_grp, n_y, n_z
        self.mats, self.offset = mats, offset
        self.plane = n_grp * n_y
        self.per, self.owners = shares(self.plane, mats)
        self.snd, self.rcv, self.part, self.zrcv, self.all, self.sems = scratch
        self.g = lax.axis_index("grp")
        slab = lax.axis_index("slab")
        self.y, self.z = slab // n_z, lax.rem(slab, n_z)
        self.q = self.g * n_y + self.y
        self.block = lax.rem(self.q + self.plane - offset, self.plane)
        self.is_owner = self.block < self.owners

    def device(self, q, z):
        return (q // self.n_y, lax.rem(q, self.n_y) * self.n_z + z)

    def copy(self, src, dst, phase, to):
        return pltpu.make_async_remote_copy(
            src_ref=src,
            dst_ref=dst,
            send_sem=self.sems.at[2 * phase],
            recv_sem=self.sems.at[2 * phase + 1],
            device_id=to,
            device_id_type=MESH,
        )

    def share(self, grads):
        tiles = 8
        for m in range(self.mats):
            low = grads[m].astype(BF16)
            for t in range(tiles):
                b = m * tiles + t
                self.snd[b // self.per, b % self.per] = low[t * 16 : (t + 1) * 16]

        for slot, (dg, dy) in enumerate(self.far_first()):
            to_g, to_y = lax.rem(self.g + dg, self.n_grp), lax.rem(self.y + dy, self.n_y)
            to = to_g * self.n_y + to_y
            block = lax.rem(to + self.plane - self.offset, self.plane)

            @pl.when(block < self.owners)
            def _():
                self.copy(
                    self.snd.at[block], self.rcv.at[slot], 0, (to_g, to_y * self.n_z + self.z)
                ).start()

    def far_first(self):
        def hops(step):
            chips = (step[0] + 1) // 2
            return min(chips, self.n_grp // 2 - chips) + min(step[1], self.n_y - step[1])

        places = [(dg, dy) for dg in range(self.n_grp) for dy in range(self.n_y) if dg or dy]
        return sorted(places, key=hops, reverse=True)

    def line(self):
        @pl.when(self.is_owner)
        def _():
            others = self.plane - 1
            bytes_of(self.rcv.at[pl.ds(0, others)], self.sems.at[1]).wait()
            total = self.snd[self.block].astype(F32)
            for i in range(others):
                total = total + self.rcv[i].astype(F32)
            self.part[0] = total.astype(BF16)
            self.zrcv[self.n_z - 1] = total.astype(BF16)
            for t in sorted(range(1, self.n_z), key=lambda t: -min(t, self.n_z - t)):
                to = lax.rem(self.z + t, self.n_z)
                self.copy(
                    self.part.at[0], self.zrcv.at[self.n_z - 1 - t], 1, self.device(self.q, to)
                ).start()

    def spread(self):
        @pl.when(self.is_owner)
        def _():
            bytes_of(self.zrcv.at[pl.ds(0, self.n_z - 1)], self.sems.at[3]).wait()
            total = jnp.zeros(self.part.shape[1:], F32)
            for i in range(self.n_z):
                total = total + self.zrcv[self.slot_of(i)].astype(F32)
            self.part[1] = total.astype(BF16)
            self.all[self.block] = total.astype(BF16)

            for dg, dy in self.far_first():
                to = (
                    lax.rem(self.g + dg, self.n_grp),
                    lax.rem(self.y + dy, self.n_y) * self.n_z + self.z,
                )
                self.copy(self.part.at[1], self.all.at[self.block], 2, to).start()

    def slot_of(self, i):
        return lax.rem(self.n_z - 1 - (self.z - i) + 2 * self.n_z, self.n_z)

    def finish(self, out, first):
        own = self.is_owner

        @pl.when(own)
        def _():
            bytes_of(self.snd.at[pl.ds(0, self.owners - 1)], self.sems.at[0]).wait()
            bytes_of(self.zrcv.at[pl.ds(0, self.n_z - 1)], self.sems.at[2]).wait()
            bytes_of(self.rcv.at[pl.ds(0, self.plane - 1)], self.sems.at[4]).wait()
            if self.owners > 1:
                bytes_of(self.all.at[pl.ds(0, self.owners - 1)], self.sems.at[5]).wait()

        @pl.when(jnp.logical_not(own))
        def _():
            bytes_of(self.snd.at[pl.ds(0, self.owners)], self.sems.at[0]).wait()
            bytes_of(self.all.at[pl.ds(0, self.owners)], self.sems.at[5]).wait()

        for m in range(self.mats):
            tiles = []
            for t in range(8):
                b = m * 8 + t
                tiles.append(self.all[b // self.per, b % self.per])
            total = jnp.concatenate(tiles, axis=0).astype(F32)
            square = jnp.sum(jnp.sum(total * total, axis=0, keepdims=True), axis=1, keepdims=True)
            out[first + m] = total / jnp.sqrt(square * (1.0 / (128 * 128)) + 1e-06)


def shares(plane, mats):
    blocks = mats * 8
    per = -(-blocks // plane)
    while blocks % per:
        per += 1
    return per, blocks // per


def sum_scratch(plane, n_z, mats):
    per, owners = shares(plane, mats)
    return [
        pltpu.VMEM((owners, per, 16, 128), BF16),
        pltpu.VMEM((plane, per, 16, 128), BF16),
        pltpu.VMEM((2, per, 16, 128), BF16),
        pltpu.VMEM((n_z, per, 16, 128), BF16),
        pltpu.VMEM((owners, per, 16, 128), BF16),
        pltpu.SemaphoreType.DMA((6,)),
    ]


N_IN = 13
CH = 16


def kernel(n_grp, n_y, n_z, dims, *refs):
    rows, slots, migr, halo = dims
    table_rows = rows + 2 * halo
    ins = refs[:N_IN]
    updated_ref, grad_ref, steps_ref = refs[N_IN : N_IN + 3]
    scratch = refs[N_IN + 3 :]
    held = scratch[:N_IN]
    (
        in_sems,
        halo_sems,
        y_sem,
        two_sem,
        four_sem,
        snd,
        rcv,
        far_rows,
        table,
        ret_snd,
        ret_rcv,
        row,
        oh,
        oht,
        mask,
        neigh,
        centre,
        agg,
        hid,
        ds1,
        md,
        d_agg,
        d_centre,
        d_neigh,
        g_msg,
    ) = scratch[N_IN : N_IN + 25]
    reduce_scratch = scratch[N_IN + 25 :]
    (nodes, leave, arrive, send, nbr, valid, w_send, w_recv, w_msg, w_self, w_agg, w_out, cot) = held

    g, slab = lax.axis_index("grp"), lax.axis_index("slab")
    n_slab = n_y * n_z
    y, z = slab // n_z, lax.rem(slab, n_z)
    plane = n_grp * n_y
    q = g * n_y + y
    lower = (g, lax.rem(slab + n_slab - 1, n_slab))
    upper = (g, lax.rem(slab + 1, n_slab))
    lower2 = (g, lax.rem(slab + n_slab - 2, n_slab))
    upper2 = (g, lax.rem(slab + 2, n_slab))

    loads = [pltpu.make_async_copy(ins[i], held[i], in_sems.at[i]) for i in range(N_IN)]
    for i in range(N_IN):
        loads[i].start()

    def along(dy, dz):
        return (g, lax.rem(y + dy, n_y) * n_z + lax.rem(z + dz, n_z))

    def steps(distances, size):
        return sorted({d % size for d in distances} - {0})

    near = [lower, upper, lower2, upper2]
    near += [(lax.rem(g + d, n_grp), slab) for d in range(1, n_grp)]
    near += [along(d, 0) for d in range(1, n_y)]
    near += [along(0, d) for d in steps((1, -1, 2, -2), n_z)]
    barrier = pltpu.get_barrier_semaphore()
    for to in near:
        pl.semaphore_signal(barrier, inc=1, device_id=to, device_id_type=MESH)

    def pass_on(sem, targets):
        for to in targets:
            pl.semaphore_signal(sem, inc=1, device_id=to, device_id_type=MESH)

    over_y = [along(d, 0) for d in range(1, n_y)]
    two_on = [along(0, d) for d in steps((2, -2), n_z)]
    four_on = [along(0, d) for d in steps((4, -4), n_z)]

    def send_to(src, dst, k, to):
        return pltpu.make_async_remote_copy(
            src_ref=src,
            dst_ref=dst,
            send_sem=halo_sems.at[2 * k],
            recv_sem=halo_sems.at[2 * k + 1],
            device_id=to,
            device_id_type=MESH,
        )

    for i in range(4):
        loads[i].wait()
    mine = nodes[...]
    arrive_hot = hot(arrive[...], (rows + 2 * migr, rows), 0)
    send_hot = hot(send[...], (rows, 2 * halo), 0)
    moving = inner(hot(leave[...], (rows, 2 * migr), 0), mine).astype(BF16)
    chosen = dot(arrive_hot, send_hot).astype(BF16)
    lent = inner(chosen[0:rows], mine).astype(BF16)
    picks = chosen[rows:]
    down, up = moving[0:migr], moving[migr:]
    for k, (part, leaving) in enumerate(((lent[0:halo], down), (lent[halo:], up))):
        snd[k, 0:halo] = part
        snd[k, halo : halo + 2 * migr] = picks
        snd[k, halo + 2 * migr :] = leaving
    pl.semaphore_wait(barrier, len(near))
    fetching = []
    for k, (near, far) in enumerate(((lower, lower2), (upper, upper2))):
        fetching.append(send_to(snd.at[k], rcv.at[k], k, near))
        fetching.append(
            send_to(snd.at[k, pl.ds(halo + 2 * migr, migr)], far_rows.at[k], 2 + k, far)
        )
    for copy in fetching:
        copy.start()
    pass_on(y_sem, over_y)
    pass_on(two_sem, two_on)
    for i in range(4, N_IN):
        loads[i].wait()
    row[...] = jnp.where(valid[...] > 0, nbr[...], table_rows)
    across = row[...].T
    for k in range(slots):
        index = across[:, k : k + 1]
        here = pl.ds(k * rows, rows)
        oh[here, :] = hot(index, (rows, table_rows), 1)
        mask[here, :] = jnp.where(
            jnp.broadcast_to(index, (rows, 128)) < table_rows, 1.0, 0.0
        ).astype(F32)
    d_hid = by_transpose(cot[...], w_out[...])
    w_msg_half = half(w_msg[...])
    kept = inner(arrive_hot[0:rows], mine)
    for copy in fetching:
        copy.wait()

    from_below, from_above = rcv.at[1], rcv.at[0]
    low_new, high_new = from_below[halo + 2 * migr :], from_above[halo + 2 * migr :]
    moved = kept + inner(arrive_hot[rows:], jnp.concatenate([low_new, high_new], axis=0))
    moved = moved.astype(BF16)
    low_rows = inner(from_below[halo : halo + 2 * migr], jnp.concatenate([far_rows[1], down], axis=0))
    high_rows = inner(from_above[halo : halo + 2 * migr], jnp.concatenate([up, far_rows[0]], axis=0))
    table[pl.ds(0, rows)] = moved
    table[pl.ds(rows, halo)] = from_below[0:halo] + low_rows[halo:].astype(BF16)
    table[pl.ds(rows + halo, halo)] = from_above[0:halo] + high_rows[0:halo].astype(BF16)
    neigh[...] = (0.5 * dot(table[...], w_recv[...])).astype(BF16)
    centre[...] = 0.5 * dot(moved, w_send[...])

    agg[...] = jnp.zeros_like(agg)
    span = CH * rows

    def front(c, carry):
        here = pl.ds(pl.multiple_of(c * span, span), span)
        pre = dot(oh[here, :], neigh[...]) + jnp.concatenate([centre[...]] * CH, axis=0)
        act, slope = silu_pair(pre)
        low = act.astype(BF16)
        hid[here, :] = low
        ds1[here, :] = slope
        act, slope = silu_pair(dot(low, w_msg_half))
        live = mask[here, :]
        md[here, :] = live * slope
        part = live * act
        total = part[0:rows]
        for u in range(1, CH):
            total = total + part[u * rows : (u + 1) * rows]
        agg[...] += total
        return carry

    lax.fori_loop(0, slots // CH, front, 0)

    if two_on:
        pl.semaphore_wait(two_sem, len(two_on))
    pass_on(four_sem, four_on)

    moved = table[pl.ds(0, rows)]
    agg_b = agg[...].astype(BF16)
    act, slope = silu_pair(0.5 * (dot(moved, w_self[...]) + dot(agg_b, w_agg[...])))
    node_hid = act.astype(BF16)
    updated_ref[...] = (moved.astype(F32) + dot(node_hid, w_out[...])).astype(BF16)
    d_node_pre = (0.5 * d_hid * slope).astype(BF16)
    d_agg[...] = 0.5 * by_transpose(d_node_pre, w_agg[...])
    g_out = inner(node_hid, cot[...])
    g_self = inner(moved, d_node_pre)
    g_agg = inner(agg_b, d_node_pre)
    d_local = cot[...].astype(F32) + by_transpose(d_node_pre, w_self[...])

    d_centre[...] = jnp.zeros_like(d_centre)
    d_neigh[...] = jnp.zeros_like(d_neigh)
    g_msg[...] = jnp.zeros_like(g_msg)

    def back(c, carry):
        here = pl.ds(pl.multiple_of(c * span, span), span)
        for u in range(CH):
            index = row[pl.ds(c * CH + u, 1), :]
            oht[:, u * rows : (u + 1) * rows] = hot(index, (table_rows, rows), 0)
        d_pre2 = (jnp.concatenate([d_agg[...]] * CH, axis=0) * md[here, :]).astype(BF16)
        d_pre = by_transpose(d_pre2, w_msg_half) * ds1[here, :]
        g_msg[...] += inner(hid[here, :], d_pre2)
        total = d_pre[0:rows]
        for u in range(1, CH):
            total = total + d_pre[u * rows : (u + 1) * rows]
        d_centre[...] += total
        d_neigh[...] += dot(oht[...], d_pre.astype(BF16))
        return carry

    lax.fori_loop(0, slots // CH, back, 0)

    d_neigh_b = d_neigh[...].astype(BF16)
    ret_snd[...] = by_transpose(d_neigh_b[rows:], w_recv[...]).astype(BF16)
    returning = [
        send_to(ret_snd.at[pl.ds(0, halo)], ret_rcv.at[pl.ds(halo, halo)], 4, lower),
        send_to(ret_snd.at[pl.ds(halo, halo)], ret_rcv.at[pl.ds(0, halo)], 5, upper),
    ]
    for copy in returning:
        copy.start()
    d_centre_b = d_centre[...].astype(BF16)
    moved = table[pl.ds(0, rows)]
    g_send = inner(moved, d_centre_b)
    g_recv = inner(table[...], d_neigh_b)
    if over_y:
        pl.semaphore_wait(y_sem, len(over_y))
    reduce = Sum(n_grp, n_y, n_z, 6, 0, reduce_scratch)
    reduce.share([g_send, g_recv, g_msg[...], g_self, g_agg, g_out])
    d_local = d_local + by_transpose(d_centre_b, w_send[...])
    d_local = d_local + by_transpose(d_neigh_b[0:rows], w_recv[...])
    if four_on:
        pl.semaphore_wait(four_sem, len(four_on))
    reduce.line()
    for copy in returning:
        copy.wait()
    d_local = d_local + dot(send_hot, ret_rcv[...])
    grad_ref[...] = d_local.astype(BF16)
    reduce.spread()
    reduce.finish(steps_ref, 0)


def shards(n_grp, n_y, n_z, *args):
    nodes, leave_list, arrive_list, send_list, neighbours, valid = args[:6]
    weights, cotangent = args[6:12], args[12]
    operands = (
        nodes[0],
        leave_list,
        arrive_list,
        send_list,
        neighbours[0].T,
        valid[0].T,
        *weights,
        cotangent[0],
    )
    operands = [pltpu.with_memory_space_constraint(x, pltpu.HBM) for x in operands]
    rows, width = operands[0].shape
    slots = operands[4].shape[0]
    migr, halo = leave_list.shape[1] // 2, send_list.shape[1] // 2
    table_rows = rows + 2 * halo
    edges = rows * slots
    plane = n_grp * n_y
    scratch = [pltpu.VMEM(x.shape, x.dtype) for x in operands]
    scratch += [
        pltpu.SemaphoreType.DMA((N_IN,)),
        pltpu.SemaphoreType.DMA((12,)),
        pltpu.SemaphoreType.REGULAR,
        pltpu.SemaphoreType.REGULAR,
        pltpu.SemaphoreType.REGULAR,
        pltpu.VMEM((2, halo + 3 * migr, width), BF16),
        pltpu.VMEM((2, halo + 3 * migr, width), BF16),
        pltpu.VMEM((2, migr, width), BF16),
        pltpu.VMEM((table_rows, width), BF16),
        pltpu.VMEM((2 * halo, width), BF16),
        pltpu.VMEM((2 * halo, width), BF16),
        pltpu.VMEM((slots, rows), jnp.int32),
        pltpu.VMEM((edges, table_rows), BF16),
        pltpu.VMEM((table_rows, CH * rows), BF16),
        pltpu.VMEM((edges, width), F32),
        pltpu.VMEM((table_rows, width), BF16),
        pltpu.VMEM((rows, width), F32),
        pltpu.VMEM((rows, width), F32),
        pltpu.VMEM((edges, width), BF16),
        pltpu.VMEM((edges, width), F32),
        pltpu.VMEM((edges, width), F32),
        pltpu.VMEM((rows, width), F32),
        pltpu.VMEM((rows, width), F32),
        pltpu.VMEM((table_rows, width), F32),
        pltpu.VMEM((width, width), F32),
    ]
    scratch += sum_scratch(plane, n_z, 6)
    updated, grad_nodes, weight_steps = pl.pallas_call(
        functools.partial(kernel, n_grp, n_y, n_z, (rows, slots, migr, halo)),
        out_shape=(
            jax.ShapeDtypeStruct((rows, width), BF16),
            jax.ShapeDtypeStruct((rows, width), BF16),
            jax.ShapeDtypeStruct((6, width, width), F32),
        ),
        in_specs=[pl.BlockSpec(memory_space=pltpu.HBM)] * N_IN,
        out_specs=[pl.BlockSpec(memory_space=pltpu.VMEM)] * 3,
        scratch_shapes=scratch,
        compiler_params=pltpu.CompilerParams(
            collective_id=0, has_side_effects=True, vmem_limit_bytes=52 * 1024 * 1024
        ),
        name="particle_step",
    )(*operands)
    return (updated[None], grad_nodes[None], weight_steps)


def solution(mesh):
    n_grp, n_slab = mesh.shape["grp"], mesh.shape["slab"]
    n_z = 16 if n_slab > 16 else n_slab // 2
    in_specs = (
        P("grp", "slab", None),
        P("grp", "slab"),
        P("grp", "slab"),
        P("grp", "slab"),
        P("grp", "slab", None),
        P("grp", "slab", None),
        P(),
        P(),
        P(),
        P(),
        P(),
        P(),
        P("grp", "slab", None),
    )
    out_specs = (P("grp", "slab", None), P("grp", "slab", None), P())
    return jax.shard_map(
        functools.partial(shards, n_grp, n_slab // n_z, n_z),
        mesh=mesh,
        in_specs=in_specs,
        out_specs=out_specs,
        check_vma=False,
    )
```

```python
import functools

import jax
import jax.numpy as jnp
from jax import lax
from jax.experimental import pallas as pl
from jax.experimental.pallas import tpu as pltpu
from jax.sharding import PartitionSpec as P

MESH = pl.DeviceIdType.MESH
F32 = jnp.float32
BF16 = jnp.bfloat16


def silu_pair(half):
    up = 1.0 + jnp.tanh(half)
    act = half * up
    return act, up * (1.0 + (half + half) - act)


def dot(left, right):
    return lax.dot_general(left, right, (((1,), (0,)), ((), ())), preferred_element_type=F32)


def inner(left, right):
    return lax.dot_general(left, right, (((0,), (0,)), ((), ())), preferred_element_type=F32)


def by_transpose(left, right):
    return lax.dot_general(left, right, (((1,), (1,)), ((), ())), preferred_element_type=F32)


def half(weights):
    return (0.5 * weights.astype(F32)).astype(BF16)


def hot(index, shape, dim):
    place = lax.broadcasted_iota(jnp.int32, shape, dim)
    return jnp.where(place == index, 1.0, 0.0).astype(BF16)


def bytes_of(ref, sem):
    return pltpu.make_async_copy(ref, ref, sem)


class Sum:
    def __init__(self, n_grp, n_y, n_z, mats, from_end, scratch):
        self.n_grp, self.n_y, self.n_z = n_grp, n_y, n_z
        self.mats = mats
        self.plane = n_grp * n_y
        self.per, self.owners = shares(self.plane, mats)
        self.offset = self.plane - self.owners if from_end else 0
        self.snd, self.rcv, self.part, self.zrcv, self.all, self.sems = scratch
        self.g = lax.axis_index("grp")
        slab = lax.axis_index("slab")
        self.y, self.z = slab // n_z, lax.rem(slab, n_z)
        self.q = self.g * n_y + self.y
        self.block = lax.rem(self.q + self.plane - self.offset, self.plane)
        self.is_owner = self.block < self.owners

    def device(self, q, z):
        return (q // self.n_y, lax.rem(q, self.n_y) * self.n_z + z)

    def copy(self, src, dst, phase, to):
        return pltpu.make_async_remote_copy(
            src_ref=src,
            dst_ref=dst,
            send_sem=self.sems.at[2 * phase],
            recv_sem=self.sems.at[2 * phase + 1],
            device_id=to,
            device_id_type=MESH,
        )

    def share(self, grads):
        tiles = 8
        for m in range(self.mats):
            low = grads[m].astype(BF16)
            for t in range(tiles):
                b = m * tiles + t
                self.snd[b // self.per, b % self.per] = low[t * 16 : (t + 1) * 16]

        for slot, (dg, dy) in enumerate(self.far_first()):
            to_g, to_y = lax.rem(self.g + dg, self.n_grp), lax.rem(self.y + dy, self.n_y)
            to = to_g * self.n_y + to_y
            block = lax.rem(to + self.plane - self.offset, self.plane)

            @pl.when(block < self.owners)
            def _():
                self.copy(
                    self.snd.at[block], self.rcv.at[slot], 0, (to_g, to_y * self.n_z + self.z)
                ).start()

    def far_first(self):
        def hops(step):
            chips = (step[0] + 1) // 2
            return min(chips, self.n_grp // 2 - chips) + min(step[1], self.n_y - step[1])

        places = [(dg, dy) for dg in range(self.n_grp) for dy in range(self.n_y) if dg or dy]
        return sorted(places, key=hops, reverse=True)

    def line(self):
        @pl.when(self.is_owner)
        def _():
            others = self.plane - 1
            bytes_of(self.rcv.at[pl.ds(0, others)], self.sems.at[1]).wait()
            total = self.snd[self.block].astype(F32)
            for i in range(others):
                total = total + self.rcv[i].astype(F32)
            self.part[0] = total.astype(BF16)
            self.zrcv[self.n_z - 1] = total.astype(BF16)
            for t in sorted(range(1, self.n_z), key=lambda t: -min(t, self.n_z - t)):
                to = lax.rem(self.z + t, self.n_z)
                self.copy(
                    self.part.at[0], self.zrcv.at[self.n_z - 1 - t], 1, self.device(self.q, to)
                ).start()

    def spread(self):
        @pl.when(self.is_owner)
        def _():
            bytes_of(self.zrcv.at[pl.ds(0, self.n_z - 1)], self.sems.at[3]).wait()
            total = jnp.zeros(self.part.shape[1:], F32)
            for i in range(self.n_z):
                total = total + self.zrcv[self.slot_of(i)].astype(F32)
            self.part[1] = total.astype(BF16)
            self.all[self.block] = total.astype(BF16)

            for dg, dy in self.far_first():
                to = (
                    lax.rem(self.g + dg, self.n_grp),
                    lax.rem(self.y + dy, self.n_y) * self.n_z + self.z,
                )
                self.copy(self.part.at[1], self.all.at[self.block], 2, to).start()

    def slot_of(self, i):
        return lax.rem(self.n_z - 1 - (self.z - i) + 2 * self.n_z, self.n_z)

    def finish(self, out, first):
        own = self.is_owner

        @pl.when(own)
        def _():
            bytes_of(self.snd.at[pl.ds(0, self.owners - 1)], self.sems.at[0]).wait()
            bytes_of(self.zrcv.at[pl.ds(0, self.n_z - 1)], self.sems.at[2]).wait()
            bytes_of(self.rcv.at[pl.ds(0, self.plane - 1)], self.sems.at[4]).wait()
            if self.owners > 1:
                bytes_of(self.all.at[pl.ds(0, self.owners - 1)], self.sems.at[5]).wait()

        @pl.when(jnp.logical_not(own))
        def _():
            bytes_of(self.snd.at[pl.ds(0, self.owners)], self.sems.at[0]).wait()
            bytes_of(self.all.at[pl.ds(0, self.owners)], self.sems.at[5]).wait()

        for m in range(self.mats):
            tiles = []
            for t in range(8):
                b = m * 8 + t
                tiles.append(self.all[b // self.per, b % self.per])
            total = jnp.concatenate(tiles, axis=0).astype(F32)
            square = jnp.sum(jnp.sum(total * total, axis=0, keepdims=True), axis=1, keepdims=True)
            out[first + m] = total / jnp.sqrt(square * (1.0 / (128 * 128)) + 1e-06)


def shares(plane, mats):
    blocks = mats * 8
    per = -(-blocks // plane)
    while blocks % per:
        per += 1
    return per, blocks // per


def sum_scratch(plane, n_z, mats):
    per, owners = shares(plane, mats)
    return [
        pltpu.VMEM((owners, per, 16, 128), BF16),
        pltpu.VMEM((plane, per, 16, 128), BF16),
        pltpu.VMEM((2, per, 16, 128), BF16),
        pltpu.VMEM((n_z, per, 16, 128), BF16),
        pltpu.VMEM((owners, per, 16, 128), BF16),
        pltpu.SemaphoreType.DMA((6,)),
    ]


N_IN = 13
CH = 16


def kernel(n_grp, n_y, n_z, dims, *refs):
    rows, slots, migr, halo = dims
    table_rows = rows + 2 * halo
    ins = refs[:N_IN]
    both_ref, steps_ref = refs[N_IN : N_IN + 2]
    updated_ref, grad_ref = both_ref.at[0], both_ref.at[1]
    scratch = refs[N_IN + 2 :]
    held = scratch[:N_IN]
    (
        in_sems,
        halo_sems,
        y_sem,
        two_sem,
        four_sem,
        snd,
        rcv,
        far_rows,
        table,
        ret_snd,
        ret_rcv,
        row,
        oh,
        oht,
        mask,
        neigh,
        centre,
        agg,
        hid,
        ds1,
        md,
        d_agg,
        d_centre,
        d_neigh,
        g_msg,
    ) = scratch[N_IN : N_IN + 25]
    reduce_scratch = scratch[N_IN + 25 :]
    (nodes, leave, arrive, send, nbr, valid, w_send, w_recv, w_msg, w_self, w_agg, w_out, cot) = held

    g, slab = lax.axis_index("grp"), lax.axis_index("slab")
    n_slab = n_y * n_z
    y, z = slab // n_z, lax.rem(slab, n_z)
    plane = n_grp * n_y
    q = g * n_y + y
    lower = (g, lax.rem(slab + n_slab - 1, n_slab))
    upper = (g, lax.rem(slab + 1, n_slab))
    lower2 = (g, lax.rem(slab + n_slab - 2, n_slab))
    upper2 = (g, lax.rem(slab + 2, n_slab))

    loads = [pltpu.make_async_copy(ins[i], held[i], in_sems.at[i]) for i in range(N_IN)]
    def along(dy, dz):
        return (g, lax.rem(y + dy, n_y) * n_z + lax.rem(z + dz, n_z))

    def steps(distances, size):
        return sorted({d % size for d in distances} - {0})

    near = [lower, upper, lower2, upper2]
    near += [(lax.rem(g + d, n_grp), slab) for d in range(1, n_grp)]
    near += [along(d, 0) for d in range(1, n_y)]
    near += [along(0, d) for d in steps((1, -1, 2, -2), n_z)]
    barrier = pltpu.get_barrier_semaphore()
    for i, to in enumerate(near):
        if i == 4:
            for load in loads[:4]:
                load.start()
        pl.semaphore_signal(barrier, inc=1, device_id=to, device_id_type=MESH)
    for load in loads[4:]:
        load.start()

    def pass_on(sem, targets):
        for to in targets:
            pl.semaphore_signal(sem, inc=1, device_id=to, device_id_type=MESH)

    over_y = [along(d, 0) for d in range(1, n_y)]
    two_on = [along(0, d) for d in steps((2, -2), n_z)]
    four_on = [along(0, d) for d in steps((4, -4), n_z)]

    def send_to(src, dst, k, to):
        return pltpu.make_async_remote_copy(
            src_ref=src,
            dst_ref=dst,
            send_sem=halo_sems.at[2 * k],
            recv_sem=halo_sems.at[2 * k + 1],
            device_id=to,
            device_id_type=MESH,
        )

    for i in range(4):
        loads[i].wait()
    mine = nodes[...]
    arrive_hot = hot(arrive[...], (rows + 2 * migr, rows), 0)
    send_hot = hot(send[...], (rows, 2 * halo), 0)
    moving = inner(hot(leave[...], (rows, 2 * migr), 0), mine).astype(BF16)
    chosen = dot(arrive_hot, send_hot).astype(BF16)
    lent = inner(chosen[0:rows], mine).astype(BF16)
    picks = chosen[rows:]
    down, up = moving[0:migr], moving[migr:]
    for k, (part, leaving) in enumerate(((lent[0:halo], down), (lent[halo:], up))):
        snd[k, 0:halo] = part
        snd[k, halo : halo + 2 * migr] = picks
        snd[k, halo + 2 * migr :] = leaving
    pl.semaphore_wait(barrier, len(near))
    fetching = []
    for k, (near, far) in enumerate(((lower, lower2), (upper, upper2))):
        fetching.append(send_to(snd.at[k], rcv.at[k], k, near))
        fetching.append(
            send_to(snd.at[k, pl.ds(halo + 2 * migr, migr)], far_rows.at[k], 2 + k, far)
        )
    for copy in fetching:
        copy.start()
    pass_on(y_sem, over_y)
    pass_on(two_sem, two_on)
    for i in range(4, N_IN):
        loads[i].wait()
    row[...] = jnp.where(valid[...] > 0, nbr[...], table_rows)
    across = row[...].T
    for k in range(slots):
        index = across[:, k : k + 1]
        here = pl.ds(k * rows, rows)
        oh[here, :] = hot(index, (rows, table_rows), 1)
        mask[here, :] = jnp.where(
            jnp.broadcast_to(index, (rows, 128)) < table_rows, 1.0, 0.0
        ).astype(F32)
    for k in range(slots):
        oht[k // CH, :, k % CH * rows : (k % CH + 1) * rows] = hot(
            row[k : k + 1, :], (table_rows, rows), 0
        )
    d_hid = by_transpose(cot[...], w_out[...])
    w_msg_half = half(w_msg[...])
    kept = inner(arrive_hot[0:rows], mine)
    for copy in fetching:
        copy.wait()

    from_below, from_above = rcv.at[1], rcv.at[0]
    low_new, high_new = from_below[halo + 2 * migr :], from_above[halo + 2 * migr :]
    moved = kept + inner(arrive_hot[rows:], jnp.concatenate([low_new, high_new], axis=0))
    moved = moved.astype(BF16)
    low_rows = inner(from_below[halo : halo + 2 * migr], jnp.concatenate([far_rows[1], down], axis=0))
    high_rows = inner(from_above[halo : halo + 2 * migr], jnp.concatenate([up, far_rows[0]], axis=0))
    table[pl.ds(0, rows)] = moved
    table[pl.ds(rows, halo)] = from_below[0:halo] + low_rows[halo:].astype(BF16)
    table[pl.ds(rows + halo, halo)] = from_above[0:halo] + high_rows[0:halo].astype(BF16)
    neigh[...] = (0.5 * dot(table[...], w_recv[...])).astype(BF16)
    centre[...] = 0.5 * dot(moved, w_send[...])

    agg[...] = jnp.zeros_like(agg)
    span = CH * rows

    def front(c, carry):
        here = pl.ds(pl.multiple_of(c * span, span), span)
        pre = dot(oh[here, :], neigh[...]) + jnp.concatenate([centre[...]] * CH, axis=0)
        act, slope = silu_pair(pre)
        low = act.astype(BF16)
        hid[here, :] = low
        ds1[here, :] = slope
        act, slope = silu_pair(dot(low, w_msg_half))
        live = mask[here, :]
        md[here, :] = live * slope
        part = live * act
        total = part[0:rows]
        for u in range(1, CH):
            total = total + part[u * rows : (u + 1) * rows]
        agg[...] += total
        return carry

    lax.fori_loop(0, slots // CH, front, 0)

    if two_on:
        pl.semaphore_wait(two_sem, len(two_on))
    pass_on(four_sem, four_on)

    moved = table[pl.ds(0, rows)]
    agg_b = agg[...].astype(BF16)
    act, slope = silu_pair(0.5 * (dot(moved, w_self[...]) + dot(agg_b, w_agg[...])))
    node_hid = act.astype(BF16)
    updated_ref[...] = (moved.astype(F32) + dot(node_hid, w_out[...])).astype(BF16)
    d_node_pre = (0.5 * d_hid * slope).astype(BF16)
    d_agg[...] = 0.5 * by_transpose(d_node_pre, w_agg[...])
    g_out = inner(node_hid, cot[...])
    g_self = inner(moved, d_node_pre)
    g_agg = inner(agg_b, d_node_pre)
    if over_y:
        pl.semaphore_wait(y_sem, len(over_y))
    early = Sum(n_grp, n_y, n_z, 3, False, reduce_scratch[:6])
    late = Sum(n_grp, n_y, n_z, 3, True, reduce_scratch[6:])
    early.share([g_self, g_agg, g_out])
    d_local = cot[...].astype(F32) + by_transpose(d_node_pre, w_self[...])

    d_centre[...] = jnp.zeros_like(d_centre)
    d_neigh[...] = jnp.zeros_like(d_neigh)
    g_msg[...] = jnp.zeros_like(g_msg)

    def back(c, carry):
        here = pl.ds(pl.multiple_of(c * span, span), span)
        d_pre2 = (jnp.concatenate([d_agg[...]] * CH, axis=0) * md[here, :]).astype(BF16)
        d_pre = by_transpose(d_pre2, w_msg_half) * ds1[here, :]
        g_msg[...] += inner(hid[here, :], d_pre2)
        total = d_pre[0:rows]
        for u in range(1, CH):
            total = total + d_pre[u * rows : (u + 1) * rows]
        d_centre[...] += total
        d_neigh[...] += dot(oht[c], d_pre.astype(BF16))
        return carry

    lax.fori_loop(0, slots // CH, back, 0)

    d_neigh_b = d_neigh[...].astype(BF16)
    d_centre_b = d_centre[...].astype(BF16)
    moved = table[pl.ds(0, rows)]
    g_recv = inner(table[...], d_neigh_b)
    g_send = inner(moved, d_centre_b)
    late.share([g_send, g_recv, g_msg[...]])
    ret_snd[...] = by_transpose(d_neigh_b[rows:], w_recv[...]).astype(BF16)
    returning = [
        send_to(ret_snd.at[pl.ds(0, halo)], ret_rcv.at[pl.ds(halo, halo)], 4, lower),
        send_to(ret_snd.at[pl.ds(halo, halo)], ret_rcv.at[pl.ds(0, halo)], 5, upper),
    ]
    for copy in returning:
        copy.start()
    if four_on:
        pl.semaphore_wait(four_sem, len(four_on))
    early.line()
    d_local = d_local + by_transpose(d_centre_b, w_send[...])
    d_local = d_local + by_transpose(d_neigh_b[0:rows], w_recv[...])
    for copy in returning:
        copy.wait()
    d_local = d_local + dot(send_hot, ret_rcv[...])
    grad_ref[...] = d_local.astype(BF16)
    late.line()
    early.spread()
    late.spread()
    early.finish(steps_ref, 3)
    late.finish(steps_ref, 0)


def shards(n_grp, n_y, n_z, *args):
    nodes, leave_list, arrive_list, send_list, neighbours, valid = args[:6]
    weights, cotangent = args[6:12], args[12]
    operands = (
        nodes[0],
        leave_list,
        arrive_list,
        send_list,
        neighbours[0].T,
        valid[0].T,
        *weights,
        cotangent[0],
    )
    operands = [pltpu.with_memory_space_constraint(x, pltpu.HBM) for x in operands]
    rows, width = operands[0].shape
    slots = operands[4].shape[0]
    migr, halo = leave_list.shape[1] // 2, send_list.shape[1] // 2
    table_rows = rows + 2 * halo
    edges = rows * slots
    plane = n_grp * n_y
    scratch = [pltpu.VMEM(x.shape, x.dtype) for x in operands]
    scratch += [
        pltpu.SemaphoreType.DMA((N_IN,)),
        pltpu.SemaphoreType.DMA((12,)),
        pltpu.SemaphoreType.REGULAR,
        pltpu.SemaphoreType.REGULAR,
        pltpu.SemaphoreType.REGULAR,
        pltpu.VMEM((2, halo + 3 * migr, width), BF16),
        pltpu.VMEM((2, halo + 3 * migr, width), BF16),
        pltpu.VMEM((2, migr, width), BF16),
        pltpu.VMEM((table_rows, width), BF16),
        pltpu.VMEM((2 * halo, width), BF16),
        pltpu.VMEM((2 * halo, width), BF16),
        pltpu.VMEM((slots, rows), jnp.int32),
        pltpu.VMEM((edges, table_rows), BF16),
        pltpu.VMEM((slots // CH, table_rows, CH * rows), BF16),
        pltpu.VMEM((edges, width), F32),
        pltpu.VMEM((table_rows, width), BF16),
        pltpu.VMEM((rows, width), F32),
        pltpu.VMEM((rows, width), F32),
        pltpu.VMEM((edges, width), BF16),
        pltpu.VMEM((edges, width), F32),
        pltpu.VMEM((edges, width), F32),
        pltpu.VMEM((rows, width), F32),
        pltpu.VMEM((rows, width), F32),
        pltpu.VMEM((table_rows, width), F32),
        pltpu.VMEM((width, width), F32),
    ]
    scratch += sum_scratch(plane, n_z, 3) + sum_scratch(plane, n_z, 3)
    both, weight_steps = pl.pallas_call(
        functools.partial(kernel, n_grp, n_y, n_z, (rows, slots, migr, halo)),
        out_shape=(
            jax.ShapeDtypeStruct((2, rows, width), BF16),
            jax.ShapeDtypeStruct((6, width, width), F32),
        ),
        in_specs=[pl.BlockSpec(memory_space=pltpu.HBM)] * N_IN,
        out_specs=[pl.BlockSpec(memory_space=pltpu.VMEM)] * 2,
        scratch_shapes=scratch,
        compiler_params=pltpu.CompilerParams(
            collective_id=0, has_side_effects=True, vmem_limit_bytes=52 * 1024 * 1024
        ),
        name="particle_step",
    )(*operands)
    return (both[0][None], both[1][None], weight_steps)


def solution(mesh):
    n_grp, n_slab = mesh.shape["grp"], mesh.shape["slab"]
    n_z = 16 if n_slab > 16 else n_slab // 2
    in_specs = (
        P("grp", "slab", None),
        P("grp", "slab"),
        P("grp", "slab"),
        P("grp", "slab"),
        P("grp", "slab", None),
        P("grp", "slab", None),
        P(),
        P(),
        P(),
        P(),
        P(),
        P(),
        P("grp", "slab", None),
    )
    out_specs = (P("grp", "slab", None), P("grp", "slab", None), P())
    return jax.shard_map(
        functools.partial(shards, n_grp, n_slab // n_z, n_z),
        mesh=mesh,
        in_specs=in_specs,
        out_specs=out_specs,
        check_vma=False,
    )
```

```python
import functools

import jax
import jax.numpy as jnp
from jax import lax
from jax.experimental import pallas as pl
from jax.experimental.pallas import tpu as pltpu
from jax.sharding import PartitionSpec as P

MESH = pl.DeviceIdType.MESH
F32 = jnp.float32
BF16 = jnp.bfloat16


def silu_pair(half):
    up = 1.0 + jnp.tanh(half)
    act = half * up
    return act, up + act * (2.0 - up)


def dot(left, right):
    return lax.dot_general(left, right, (((1,), (0,)), ((), ())), preferred_element_type=F32)


def inner(left, right):
    return lax.dot_general(left, right, (((0,), (0,)), ((), ())), preferred_element_type=F32)


def by_transpose(left, right):
    return lax.dot_general(left, right, (((1,), (1,)), ((), ())), preferred_element_type=F32)


def twice(weights):
    zero = jnp.zeros_like(weights)
    return jnp.concatenate(
        [
            jnp.concatenate([weights, zero], axis=1),
            jnp.concatenate([zero, weights], axis=1),
        ],
        axis=0,
    )


def beside(rows):
    middle = rows.shape[0] // 2
    return jnp.concatenate([rows[:middle], rows[middle:]], axis=1)


def below(rows):
    middle = rows.shape[1] // 2
    return jnp.concatenate([rows[:, :middle], rows[:, middle:]], axis=0)


def half(weights):
    return (0.5 * weights.astype(F32)).astype(BF16)


def hot(index, shape, dim):
    place = lax.broadcasted_iota(jnp.int32, shape, dim)
    return jnp.where(place == index, 1.0, 0.0).astype(BF16)


def bytes_of(ref, sem):
    return pltpu.make_async_copy(ref, ref, sem)


class Sum:
    def __init__(self, n_grp, n_y, n_z, mats, from_end, scratch):
        self.n_grp, self.n_y, self.n_z = n_grp, n_y, n_z
        self.mats = mats
        self.plane = n_grp * n_y
        self.per, self.owners = shares(self.plane, mats)
        self.offset = self.plane - self.owners if from_end else 0
        self.snd, self.rcv, self.part, self.zrcv, self.all, self.sems = scratch
        self.g = lax.axis_index("grp")
        slab = lax.axis_index("slab")
        self.y, self.z = slab // n_z, lax.rem(slab, n_z)
        self.q = self.g * n_y + self.y
        self.block = lax.rem(self.q + self.plane - self.offset, self.plane)
        self.is_owner = self.block < self.owners

    def device(self, q, z):
        return (q // self.n_y, lax.rem(q, self.n_y) * self.n_z + z)

    def copy(self, src, dst, phase, to):
        return pltpu.make_async_remote_copy(
            src_ref=src,
            dst_ref=dst,
            send_sem=self.sems.at[2 * phase],
            recv_sem=self.sems.at[2 * phase + 1],
            device_id=to,
            device_id_type=MESH,
        )

    def share(self, grads):
        tiles = 8
        for m in range(self.mats):
            low = grads[m].astype(BF16)
            for t in range(tiles):
                b = m * tiles + t
                self.snd[b // self.per, b % self.per] = low[t * 16 : (t + 1) * 16]

        for slot, (dg, dy) in enumerate(self.far_first()):
            to_g, to_y = lax.rem(self.g + dg, self.n_grp), lax.rem(self.y + dy, self.n_y)
            to = to_g * self.n_y + to_y
            block = lax.rem(to + self.plane - self.offset, self.plane)

            @pl.when(block < self.owners)
            def _():
                self.copy(
                    self.snd.at[block], self.rcv.at[slot], 0, (to_g, to_y * self.n_z + self.z)
                ).start()

    def far_first(self):
        def hops(step):
            chips = (step[0] + 1) // 2
            return min(chips, self.n_grp // 2 - chips) + min(step[1], self.n_y - step[1])

        places = [(dg, dy) for dg in range(self.n_grp) for dy in range(self.n_y) if dg or dy]
        return sorted(places, key=hops, reverse=True)

    def line(self):
        @pl.when(self.is_owner)
        def _():
            others = self.plane - 1
            bytes_of(self.rcv.at[pl.ds(0, others)], self.sems.at[1]).wait()
            total = self.snd[self.block].astype(F32)
            for i in range(others):
                total = total + self.rcv[i].astype(F32)
            self.part[0] = total.astype(BF16)
            self.zrcv[self.n_z - 1] = total.astype(BF16)
            for t in sorted(range(1, self.n_z), key=lambda t: -min(t, self.n_z - t)):
                to = lax.rem(self.z + t, self.n_z)
                self.copy(
                    self.part.at[0], self.zrcv.at[self.n_z - 1 - t], 1, self.device(self.q, to)
                ).start()

    def spread(self):
        @pl.when(self.is_owner)
        def _():
            bytes_of(self.zrcv.at[pl.ds(0, self.n_z - 1)], self.sems.at[3]).wait()
            total = jnp.zeros(self.part.shape[1:], F32)
            for i in range(self.n_z):
                total = total + self.zrcv[self.slot_of(i)].astype(F32)
            self.part[1] = total.astype(BF16)
            self.all[self.block] = total.astype(BF16)

            for dg, dy in self.far_first():
                to = (
                    lax.rem(self.g + dg, self.n_grp),
                    lax.rem(self.y + dy, self.n_y) * self.n_z + self.z,
                )
                self.copy(self.part.at[1], self.all.at[self.block], 2, to).start()

    def slot_of(self, i):
        return lax.rem(self.n_z - 1 - (self.z - i) + 2 * self.n_z, self.n_z)

    def finish(self, out, first):
        own = self.is_owner

        @pl.when(own)
        def _():
            bytes_of(self.snd.at[pl.ds(0, self.owners - 1)], self.sems.at[0]).wait()
            bytes_of(self.zrcv.at[pl.ds(0, self.n_z - 1)], self.sems.at[2]).wait()
            bytes_of(self.rcv.at[pl.ds(0, self.plane - 1)], self.sems.at[4]).wait()
            if self.owners > 1:
                bytes_of(self.all.at[pl.ds(0, self.owners - 1)], self.sems.at[5]).wait()

        @pl.when(jnp.logical_not(own))
        def _():
            bytes_of(self.snd.at[pl.ds(0, self.owners)], self.sems.at[0]).wait()
            bytes_of(self.all.at[pl.ds(0, self.owners)], self.sems.at[5]).wait()

        for m in range(self.mats):
            tiles = []
            for t in range(8):
                b = m * 8 + t
                tiles.append(self.all[b // self.per, b % self.per])
            total = jnp.concatenate(tiles, axis=0).astype(F32)
            square = jnp.sum(jnp.sum(total * total, axis=0, keepdims=True), axis=1, keepdims=True)
            out[first + m] = total / jnp.sqrt(square * (1.0 / (128 * 128)) + 1e-06)


def shares(plane, mats):
    blocks = mats * 8
    per = -(-blocks // plane)
    while blocks % per:
        per += 1
    return per, blocks // per


def sum_scratch(plane, n_z, mats):
    per, owners = shares(plane, mats)
    return [
        pltpu.VMEM((owners, per, 16, 128), BF16),
        pltpu.VMEM((plane, per, 16, 128), BF16),
        pltpu.VMEM((2, per, 16, 128), BF16),
        pltpu.VMEM((n_z, per, 16, 128), BF16),
        pltpu.VMEM((owners, per, 16, 128), BF16),
        pltpu.SemaphoreType.DMA((6,)),
    ]


N_IN = 13
CH = 16


def kernel(n_grp, n_y, n_z, dims, *refs):
    rows, slots, migr, halo = dims
    table_rows = rows + 2 * halo
    ins = refs[:N_IN]
    both_ref, steps_ref = refs[N_IN : N_IN + 2]
    updated_ref, grad_ref = both_ref.at[0], both_ref.at[1]
    scratch = refs[N_IN + 2 :]
    held = scratch[:N_IN]
    (
        in_sems,
        halo_sems,
        y_sem,
        two_sem,
        four_sem,
        w_pair,
        w_half,
        left,
        snd,
        rcv,
        far_rows,
        table,
        ret_snd,
        ret_rcv,
        row,
        oh,
        oht,
        mask,
        neigh,
        centre,
        agg,
        hid,
        ds1,
        md,
        d_agg,
        d_centre,
        d_neigh,
        g_msg,
    ) = scratch[N_IN : N_IN + 28]
    reduce_scratch = scratch[N_IN + 28 :]
    (nodes, leave, arrive, send, nbr, valid, w_send, w_recv, w_msg, w_self, w_agg, w_out, cot) = held

    g, slab = lax.axis_index("grp"), lax.axis_index("slab")
    n_slab = n_y * n_z
    y, z = slab // n_z, lax.rem(slab, n_z)
    plane = n_grp * n_y
    q = g * n_y + y
    lower = (g, lax.rem(slab + n_slab - 1, n_slab))
    upper = (g, lax.rem(slab + 1, n_slab))
    lower2 = (g, lax.rem(slab + n_slab - 2, n_slab))
    upper2 = (g, lax.rem(slab + 2, n_slab))

    loads = [pltpu.make_async_copy(ins[i], held[i], in_sems.at[i]) for i in range(N_IN)]
    def along(dy, dz):
        return (g, lax.rem(y + dy, n_y) * n_z + lax.rem(z + dz, n_z))

    def steps(distances, size):
        return sorted({d % size for d in distances} - {0})

    near = [lower, upper, lower2, upper2]
    near += [(lax.rem(g + d, n_grp), slab) for d in range(1, n_grp)]
    near += [along(d, 0) for d in range(1, n_y)]
    near += [along(0, d) for d in steps((1, -1, 2, -2), n_z)]
    barrier = pltpu.get_barrier_semaphore()
    for i, to in enumerate(near):
        if i == 4:
            for load in loads[:4]:
                load.start()
        pl.semaphore_signal(barrier, inc=1, device_id=to, device_id_type=MESH)
    for load in loads[4:]:
        load.start()

    def pass_on(sem, targets):
        for to in targets:
            pl.semaphore_signal(sem, inc=1, device_id=to, device_id_type=MESH)

    over_y = [along(d, 0) for d in range(1, n_y)]
    two_on = [along(0, d) for d in steps((2, -2), n_z)]
    four_on = [along(0, d) for d in steps((4, -4), n_z)]

    def send_to(src, dst, k, to):
        return pltpu.make_async_remote_copy(
            src_ref=src,
            dst_ref=dst,
            send_sem=halo_sems.at[2 * k],
            recv_sem=halo_sems.at[2 * k + 1],
            device_id=to,
            device_id_type=MESH,
        )

    for i in range(4):
        loads[i].wait()
    mine = nodes[...]
    arrive_hot = hot(arrive[...], (rows + 2 * migr, rows), 0)
    send_hot = hot(send[...], (rows, 2 * halo), 0)
    moving = inner(hot(leave[...], (rows, 2 * migr), 0), mine).astype(BF16)
    chosen = dot(arrive_hot, send_hot).astype(BF16)
    lent = inner(chosen[0:rows], mine).astype(BF16)
    picks = chosen[rows:]
    down, up = moving[0:migr], moving[migr:]
    for k, (part, leaving) in enumerate(((lent[0:halo], down), (lent[halo:], up))):
        snd[k, 0:halo] = part
        snd[k, halo : halo + 2 * migr] = picks
        snd[k, halo + 2 * migr :] = leaving
    pl.semaphore_wait(barrier, len(near))
    fetching = []
    for k, (near, far) in enumerate(((lower, lower2), (upper, upper2))):
        fetching.append(
            send_to(snd.at[k, pl.ds(halo + 2 * migr, migr)], far_rows.at[k], 2 + k, far)
        )
        fetching.append(send_to(snd.at[k], rcv.at[k], k, near))
    for copy in fetching:
        copy.start()
    pass_on(y_sem, over_y)
    pass_on(two_sem, two_on)
    for i in range(4, N_IN):
        loads[i].wait()
    row[...] = jnp.where(valid[...] > 0, nbr[...], table_rows)
    across = row[...].T
    middle = table_rows // 2
    for k in range(slots):
        index = across[:, k : k + 1]
        here = pl.ds(k * rows, rows)
        oh[here, :] = hot(index, (rows, table_rows), 1)
        index = jnp.broadcast_to(index, (rows, 128))
        mask[here, :] = jnp.where(index < table_rows, 1.0, 0.0).astype(F32)
        left[here, :] = jnp.where(index < middle, 1.0, 0.0).astype(BF16)
    for k in range(slots):
        index = row[k : k + 1, :]
        index = jnp.where(index >= middle, index - middle, index)
        oht[k // CH, :, k % CH * rows : (k % CH + 1) * rows] = hot(index, (middle, rows), 0)
    d_hid = by_transpose(cot[...], w_out[...])
    w_half[...] = half(w_msg[...])
    w_pair[...] = twice(w_half[...])
    kept = inner(arrive_hot[0:rows], mine)
    for copy in fetching:
        copy.wait()

    from_below, from_above = rcv.at[1], rcv.at[0]
    low_new, high_new = from_below[halo + 2 * migr :], from_above[halo + 2 * migr :]
    moved = kept + inner(arrive_hot[rows:], jnp.concatenate([low_new, high_new], axis=0))
    moved = moved.astype(BF16)
    low_rows = inner(from_below[halo : halo + 2 * migr], jnp.concatenate([far_rows[1], down], axis=0))
    high_rows = inner(from_above[halo : halo + 2 * migr], jnp.concatenate([up, far_rows[0]], axis=0))
    table[pl.ds(0, rows)] = moved
    table[pl.ds(rows, halo)] = from_below[0:halo] + low_rows[halo:].astype(BF16)
    table[pl.ds(rows + halo, halo)] = from_above[0:halo] + high_rows[0:halo].astype(BF16)
    neigh[...] = (0.5 * dot(table[...], w_recv[...])).astype(BF16)
    centre[...] = 0.5 * dot(moved, w_send[...])

    agg[...] = jnp.zeros_like(agg)
    span = CH * rows

    def front(c):
        here = pl.ds(c * span, span)
        pre = dot(oh[here, :], neigh[...]) + jnp.concatenate([centre[...]] * CH, axis=0)
        act, slope = silu_pair(pre)
        low = act.astype(BF16)
        hid[here, :] = low
        ds1[here, :] = slope
        act, slope = silu_pair(below(dot(beside(low), w_pair[...])))
        live = mask[here, :]
        md[here, :] = live * slope
        part = live * act
        total = part[0:rows]
        for u in range(1, CH):
            total = total + part[u * rows : (u + 1) * rows]
        agg[...] += total

    for c in range(slots // CH):
        front(c)

    if two_on:
        pl.semaphore_wait(two_sem, len(two_on))
    pass_on(four_sem, four_on)

    moved = table[pl.ds(0, rows)]
    agg_b = agg[...].astype(BF16)
    act, slope = silu_pair(0.5 * (dot(moved, w_self[...]) + dot(agg_b, w_agg[...])))
    node_hid = act.astype(BF16)
    updated_ref[...] = (moved.astype(F32) + dot(node_hid, w_out[...])).astype(BF16)
    d_node_pre = (0.5 * d_hid * slope).astype(BF16)
    d_agg[...] = 0.5 * by_transpose(d_node_pre, w_agg[...])
    g_out = inner(node_hid, cot[...])
    g_self = inner(moved, d_node_pre)
    g_agg = inner(agg_b, d_node_pre)
    if over_y:
        pl.semaphore_wait(y_sem, len(over_y))
    early = Sum(n_grp, n_y, n_z, 3, False, reduce_scratch[:6])
    late = Sum(n_grp, n_y, n_z, 3, True, reduce_scratch[6:])
    early.share([g_self, g_agg, g_out])
    d_local = cot[...].astype(F32) + by_transpose(d_node_pre, w_self[...])

    d_centre[...] = jnp.zeros_like(d_centre)
    d_neigh[...] = jnp.zeros_like(d_neigh)
    g_msg[...] = jnp.zeros_like(g_msg)

    def back(c):
        here = pl.ds(c * span, span)
        d_pre2 = (jnp.concatenate([d_agg[...]] * CH, axis=0) * md[here, :]).astype(BF16)
        d_pre = by_transpose(d_pre2, w_half[...]) * ds1[here, :]
        g_msg[...] += inner(hid[here, :], d_pre2)
        total = d_pre[0:rows]
        for u in range(1, CH):
            total = total + d_pre[u * rows : (u + 1) * rows]
        d_centre[...] += total
        low = d_pre.astype(BF16)
        first = low * left[here, :]
        sides = jnp.concatenate([first, low - first], axis=1)
        d_neigh[...] += dot(oht[c], sides)

    for c in range(slots // CH):
        back(c)

    d_neigh_b = below(d_neigh[...]).astype(BF16)
    d_centre_b = d_centre[...].astype(BF16)
    moved = table[pl.ds(0, rows)]
    g_recv = inner(table[...], d_neigh_b)
    g_send = inner(moved, d_centre_b)
    late.share([g_send, g_recv, g_msg[...]])
    ret_snd[...] = by_transpose(d_neigh_b[rows:], w_recv[...]).astype(BF16)
    returning = [
        send_to(ret_snd.at[pl.ds(0, halo)], ret_rcv.at[pl.ds(halo, halo)], 4, lower),
        send_to(ret_snd.at[pl.ds(halo, halo)], ret_rcv.at[pl.ds(0, halo)], 5, upper),
    ]
    for copy in returning:
        copy.start()
    if four_on:
        pl.semaphore_wait(four_sem, len(four_on))
    early.line()
    d_local = d_local + by_transpose(d_centre_b, w_send[...])
    d_local = d_local + by_transpose(d_neigh_b[0:rows], w_recv[...])
    for copy in returning:
        copy.wait()
    d_local = d_local + dot(send_hot, ret_rcv[...])
    grad_ref[...] = d_local.astype(BF16)
    late.line()
    early.spread()
    late.spread()
    early.finish(steps_ref, 3)
    late.finish(steps_ref, 0)


def shards(n_grp, n_y, n_z, *args):
    nodes, leave_list, arrive_list, send_list, neighbours, valid = args[:6]
    weights, cotangent = args[6:12], args[12]
    operands = (
        nodes[0],
        leave_list,
        arrive_list,
        send_list,
        neighbours[0].T,
        valid[0].T,
        *weights,
        cotangent[0],
    )
    operands = [pltpu.with_memory_space_constraint(x, pltpu.HBM) for x in operands]
    rows, width = operands[0].shape
    slots = operands[4].shape[0]
    migr, halo = leave_list.shape[1] // 2, send_list.shape[1] // 2
    table_rows = rows + 2 * halo
    edges = rows * slots
    plane = n_grp * n_y
    scratch = [pltpu.VMEM(x.shape, x.dtype) for x in operands]
    scratch += [
        pltpu.SemaphoreType.DMA((N_IN,)),
        pltpu.SemaphoreType.DMA((12,)),
        pltpu.SemaphoreType.REGULAR,
        pltpu.SemaphoreType.REGULAR,
        pltpu.SemaphoreType.REGULAR,
        pltpu.VMEM((2 * width, 2 * width), BF16),
        pltpu.VMEM((width, width), BF16),
        pltpu.VMEM((edges, width), BF16),
        pltpu.VMEM((2, halo + 3 * migr, width), BF16),
        pltpu.VMEM((2, halo + 3 * migr, width), BF16),
        pltpu.VMEM((2, migr, width), BF16),
        pltpu.VMEM((table_rows, width), BF16),
        pltpu.VMEM((2 * halo, width), BF16),
        pltpu.VMEM((2 * halo, width), BF16),
        pltpu.VMEM((slots, rows), jnp.int32),
        pltpu.VMEM((edges, table_rows), BF16),
        pltpu.VMEM((slots // CH, table_rows // 2, CH * rows), BF16),
        pltpu.VMEM((edges, width), F32),
        pltpu.VMEM((table_rows, width), BF16),
        pltpu.VMEM((rows, width), F32),
        pltpu.VMEM((rows, width), F32),
        pltpu.VMEM((edges, width), BF16),
        pltpu.VMEM((edges, width), F32),
        pltpu.VMEM((edges, width), F32),
        pltpu.VMEM((rows, width), F32),
        pltpu.VMEM((rows, width), F32),
        pltpu.VMEM((table_rows // 2, 2 * width), F32),
        pltpu.VMEM((width, width), F32),
    ]
    scratch += sum_scratch(plane, n_z, 3) + sum_scratch(plane, n_z, 3)
    both, weight_steps = pl.pallas_call(
        functools.partial(kernel, n_grp, n_y, n_z, (rows, slots, migr, halo)),
        out_shape=(
            jax.ShapeDtypeStruct((2, rows, width), BF16),
            jax.ShapeDtypeStruct((6, width, width), F32),
        ),
        in_specs=[pl.BlockSpec(memory_space=pltpu.HBM)] * N_IN,
        out_specs=[pl.BlockSpec(memory_space=pltpu.VMEM)] * 2,
        scratch_shapes=scratch,
        compiler_params=pltpu.CompilerParams(
            collective_id=0, has_side_effects=True, vmem_limit_bytes=52 * 1024 * 1024
        ),
        name="particle_step",
    )(*operands)
    return (both[0][None], both[1][None], weight_steps)


def solution(mesh):
    n_grp, n_slab = mesh.shape["grp"], mesh.shape["slab"]
    n_z = 16 if n_slab > 16 else n_slab // 2
    in_specs = (
        P("grp", "slab", None),
        P("grp", "slab"),
        P("grp", "slab"),
        P("grp", "slab"),
        P("grp", "slab", None),
        P("grp", "slab", None),
        P(),
        P(),
        P(),
        P(),
        P(),
        P(),
        P("grp", "slab", None),
    )
    out_specs = (P("grp", "slab", None), P("grp", "slab", None), P())
    return jax.shard_map(
        functools.partial(shards, n_grp, n_slab // n_z, n_z),
        mesh=mesh,
        in_specs=in_specs,
        out_specs=out_specs,
        check_vma=False,
    )
```

```python
import functools

import jax
import jax.numpy as jnp
from jax import lax
from jax.experimental import pallas as pl
from jax.experimental.pallas import tpu as pltpu
from jax.sharding import PartitionSpec as P

MESH = pl.DeviceIdType.MESH
F32 = jnp.float32
BF16 = jnp.bfloat16


def silu_pair(half):
    up = 1.0 + jnp.tanh(half)
    act = half * up
    return act, up + act * (2.0 - up)


def dot(left, right):
    return lax.dot_general(left, right, (((1,), (0,)), ((), ())), preferred_element_type=F32)


def inner(left, right):
    return lax.dot_general(left, right, (((0,), (0,)), ((), ())), preferred_element_type=F32)


def by_transpose(left, right):
    return lax.dot_general(left, right, (((1,), (1,)), ((), ())), preferred_element_type=F32)


def twice(weights):
    zero = jnp.zeros_like(weights)
    return jnp.concatenate(
        [
            jnp.concatenate([weights, zero], axis=1),
            jnp.concatenate([zero, weights], axis=1),
        ],
        axis=0,
    )


def beside(rows):
    middle = rows.shape[0] // 2
    return jnp.concatenate([rows[:middle], rows[middle:]], axis=1)


def below(rows):
    middle = rows.shape[1] // 2
    return jnp.concatenate([rows[:, :middle], rows[:, middle:]], axis=0)


def half(weights):
    return (0.5 * weights.astype(F32)).astype(BF16)


def hot(index, shape, dim):
    place = lax.broadcasted_iota(jnp.int32, shape, dim)
    return jnp.where(place == index, 1.0, 0.0).astype(BF16)


def bytes_of(ref, sem):
    return pltpu.make_async_copy(ref, ref, sem)


class Sum:
    def __init__(self, n_grp, n_y, n_z, mats, least, from_end, scratch):
        self.n_grp, self.n_y, self.n_z = n_grp, n_y, n_z
        self.mats = mats
        self.plane = n_grp * n_y
        self.per, self.owners = shares(self.plane, mats, least)
        self.offset = self.plane - self.owners if from_end else 0
        self.snd, self.rcv, self.part, self.zrcv, self.all, self.sems = scratch
        self.g = lax.axis_index("grp")
        slab = lax.axis_index("slab")
        self.y, self.z = slab // n_z, lax.rem(slab, n_z)
        self.q = self.g * n_y + self.y
        self.block = lax.rem(self.q + self.plane - self.offset, self.plane)
        self.is_owner = self.block < self.owners

    def device(self, q, z):
        return (q // self.n_y, lax.rem(q, self.n_y) * self.n_z + z)

    def copy(self, src, dst, phase, to):
        return pltpu.make_async_remote_copy(
            src_ref=src,
            dst_ref=dst,
            send_sem=self.sems.at[2 * phase],
            recv_sem=self.sems.at[2 * phase + 1],
            device_id=to,
            device_id_type=MESH,
        )

    def share(self, grads):
        tiles = 8
        for m in range(self.mats):
            low = grads[m].astype(BF16)
            for t in range(tiles):
                b = m * tiles + t
                self.snd[b // self.per, b % self.per] = low[t * 16 : (t + 1) * 16]

        for slot, (dg, dy) in enumerate(self.far_first()):
            to_g, to_y = lax.rem(self.g + dg, self.n_grp), lax.rem(self.y + dy, self.n_y)
            to = to_g * self.n_y + to_y
            block = lax.rem(to + self.plane - self.offset, self.plane)

            @pl.when(block < self.owners)
            def _():
                self.copy(
                    self.snd.at[block], self.rcv.at[slot], 0, (to_g, to_y * self.n_z + self.z)
                ).start()

    def far_first(self):
        def hops(step):
            chips = (step[0] + 1) // 2
            return min(chips, self.n_grp // 2 - chips) + min(step[1], self.n_y - step[1])

        places = [(dg, dy) for dg in range(self.n_grp) for dy in range(self.n_y) if dg or dy]
        return sorted(places, key=hops, reverse=True)

    def line(self):
        @pl.when(self.is_owner)
        def _():
            others = self.plane - 1
            bytes_of(self.rcv.at[pl.ds(0, others)], self.sems.at[1]).wait()
            total = self.snd[self.block].astype(F32)
            for i in range(others):
                total = total + self.rcv[i].astype(F32)
            self.part[0] = total.astype(BF16)
            self.zrcv[self.n_z - 1] = total.astype(BF16)
            for t in sorted(range(1, self.n_z), key=lambda t: -min(t, self.n_z - t)):
                to = lax.rem(self.z + t, self.n_z)
                self.copy(
                    self.part.at[0], self.zrcv.at[self.n_z - 1 - t], 1, self.device(self.q, to)
                ).start()

    def spread(self):
        @pl.when(self.is_owner)
        def _():
            bytes_of(self.zrcv.at[pl.ds(0, self.n_z - 1)], self.sems.at[3]).wait()
            total = jnp.zeros(self.part.shape[1:], F32)
            for i in range(self.n_z):
                total = total + self.zrcv[self.slot_of(i)].astype(F32)
            self.part[1] = total.astype(BF16)
            self.all[self.block] = total.astype(BF16)

            for dg, dy in self.far_first():
                to = (
                    lax.rem(self.g + dg, self.n_grp),
                    lax.rem(self.y + dy, self.n_y) * self.n_z + self.z,
                )
                self.copy(self.part.at[1], self.all.at[self.block], 2, to).start()

    def slot_of(self, i):
        return lax.rem(self.n_z - 1 - (self.z - i) + 2 * self.n_z, self.n_z)

    def finish(self, out, first):
        own = self.is_owner

        @pl.when(own)
        def _():
            bytes_of(self.snd.at[pl.ds(0, self.owners - 1)], self.sems.at[0]).wait()
            bytes_of(self.zrcv.at[pl.ds(0, self.n_z - 1)], self.sems.at[2]).wait()
            bytes_of(self.rcv.at[pl.ds(0, self.plane - 1)], self.sems.at[4]).wait()
            if self.owners > 1:
                bytes_of(self.all.at[pl.ds(0, self.owners - 1)], self.sems.at[5]).wait()

        @pl.when(jnp.logical_not(own))
        def _():
            bytes_of(self.snd.at[pl.ds(0, self.owners)], self.sems.at[0]).wait()
            bytes_of(self.all.at[pl.ds(0, self.owners)], self.sems.at[5]).wait()

        for m in range(self.mats):
            tiles = []
            for t in range(8):
                b = m * 8 + t
                tiles.append(self.all[b // self.per, b % self.per])
            total = jnp.concatenate(tiles, axis=0).astype(F32)
            square = jnp.sum(jnp.sum(total * total, axis=0, keepdims=True), axis=1, keepdims=True)
            out[first + m] = total / jnp.sqrt(square * (1.0 / (128 * 128)) + 1e-06)


def shares(plane, mats, least):
    blocks = mats * 8
    per = max(-(-blocks // plane), least)
    while blocks % per:
        per += 1
    return per, blocks // per


def sum_scratch(plane, n_z, mats, least):
    per, owners = shares(plane, mats, least)
    return [
        pltpu.VMEM((owners, per, 16, 128), BF16),
        pltpu.VMEM((plane, per, 16, 128), BF16),
        pltpu.VMEM((2, per, 16, 128), BF16),
        pltpu.VMEM((n_z, per, 16, 128), BF16),
        pltpu.VMEM((owners, per, 16, 128), BF16),
        pltpu.SemaphoreType.DMA((6,)),
    ]


NO_EDGE = -1e30
N_IN = 13
CH = 16


def kernel(n_grp, n_y, n_z, dims, *refs):
    rows, slots, migr, halo = dims
    table_rows = rows + 2 * halo
    ins = refs[:N_IN]
    both_ref, steps_ref = refs[N_IN : N_IN + 2]
    updated_ref, grad_ref = both_ref.at[0], both_ref.at[1]
    scratch = refs[N_IN + 2 :]
    held = scratch[:N_IN]
    (
        in_sems,
        halo_sems,
        y_sem,
        two_sem,
        four_sem,
        w_pair,
        w_half,
        left,
        snd,
        rcv,
        far_rows,
        table,
        ret_snd,
        ret_rcv,
        row,
        oh,
        oht,
        mask,
        neigh,
        centre,
        agg,
        hid,
        ds1,
        md,
        d_agg,
        d_centre,
        d_neigh,
        g_msg,
    ) = scratch[N_IN : N_IN + 28]
    reduce_scratch = scratch[N_IN + 28 :]
    (nodes, leave, arrive, send, nbr, valid, w_send, w_recv, w_msg, w_self, w_agg, w_out, cot) = held

    g, slab = lax.axis_index("grp"), lax.axis_index("slab")
    n_slab = n_y * n_z
    y, z = slab // n_z, lax.rem(slab, n_z)
    plane = n_grp * n_y
    q = g * n_y + y
    lower = (g, lax.rem(slab + n_slab - 1, n_slab))
    upper = (g, lax.rem(slab + 1, n_slab))
    lower2 = (g, lax.rem(slab + n_slab - 2, n_slab))
    upper2 = (g, lax.rem(slab + 2, n_slab))

    loads = [pltpu.make_async_copy(ins[i], held[i], in_sems.at[i]) for i in range(N_IN)]
    def along(dy, dz):
        return (g, lax.rem(y + dy, n_y) * n_z + lax.rem(z + dz, n_z))

    def steps(distances, size):
        return sorted({d % size for d in distances} - {0})

    near = [lower, upper, lower2, upper2]
    near += [(lax.rem(g + d, n_grp), slab) for d in range(1, n_grp)]
    near += [along(d, 0) for d in range(1, n_y)]
    near += [along(0, d) for d in steps((1, -1, 2, -2), n_z)]
    barrier = pltpu.get_barrier_semaphore()
    for i, to in enumerate(near):
        if i == 4:
            for load in loads[:4]:
                load.start()
        pl.semaphore_signal(barrier, inc=1, device_id=to, device_id_type=MESH)
    for load in loads[4:]:
        load.start()

    def pass_on(sem, targets):
        for to in targets:
            pl.semaphore_signal(sem, inc=1, device_id=to, device_id_type=MESH)

    over_y = [along(d, 0) for d in range(1, n_y)]
    two_on = [along(0, d) for d in steps((2, -2), n_z)]
    four_on = [along(0, d) for d in steps((4, -4), n_z)]

    def send_to(src, dst, k, to):
        return pltpu.make_async_remote_copy(
            src_ref=src,
            dst_ref=dst,
            send_sem=halo_sems.at[2 * k],
            recv_sem=halo_sems.at[2 * k + 1],
            device_id=to,
            device_id_type=MESH,
        )

    for i in range(4):
        loads[i].wait()
    mine = nodes[...]
    arrive_hot = hot(arrive[...], (rows + 2 * migr, rows), 0)
    send_hot = hot(send[...], (rows, 2 * halo), 0)
    moving = inner(hot(leave[...], (rows, 2 * migr), 0), mine).astype(BF16)
    chosen = dot(arrive_hot, send_hot).astype(BF16)
    lent = inner(chosen[0:rows], mine).astype(BF16)
    picks = chosen[rows:]
    down, up = moving[0:migr], moving[migr:]
    for k, (part, leaving) in enumerate(((lent[0:halo], down), (lent[halo:], up))):
        snd[k, 0:halo] = part
        snd[k, halo : halo + 2 * migr] = picks
        snd[k, halo + 2 * migr :] = leaving
    pl.semaphore_wait(barrier, len(near))
    fetching = []
    for k, (near, far) in enumerate(((lower, lower2), (upper, upper2))):
        fetching.append(
            send_to(snd.at[k, pl.ds(halo + 2 * migr, migr)], far_rows.at[k], 2 + k, far)
        )
        fetching.append(send_to(snd.at[k], rcv.at[k], k, near))
    for copy in fetching:
        copy.start()
    pass_on(y_sem, over_y)
    pass_on(two_sem, two_on)
    for i in range(4, N_IN):
        loads[i].wait()
    row[...] = jnp.where(valid[...] > 0, nbr[...], table_rows)
    across = row[...].T
    middle = table_rows // 2
    for k in range(slots):
        index = across[:, k : k + 1]
        here = pl.ds(k * rows, rows)
        oh[here, :] = hot(index, (rows, table_rows), 1)
        index = jnp.broadcast_to(index, (rows, 128))
        mask[here, :] = jnp.where(index < table_rows, 0.0, NO_EDGE).astype(F32)
        left[here, :] = jnp.where(index < middle, 1.0, 0.0).astype(BF16)
    for k in range(slots):
        index = row[k : k + 1, :]
        index = jnp.where(index >= middle, index - middle, index)
        oht[k // CH, :, k % CH * rows : (k % CH + 1) * rows] = hot(index, (middle, rows), 0)
    d_hid = by_transpose(cot[...], w_out[...])
    w_half[...] = half(w_msg[...])
    w_pair[...] = twice(w_half[...])
    kept = inner(arrive_hot[0:rows], mine)
    for copy in fetching:
        copy.wait()

    from_below, from_above = rcv.at[1], rcv.at[0]
    low_new, high_new = from_below[halo + 2 * migr :], from_above[halo + 2 * migr :]
    moved = kept + inner(arrive_hot[rows:], jnp.concatenate([low_new, high_new], axis=0))
    moved = moved.astype(BF16)
    low_rows = inner(from_below[halo : halo + 2 * migr], jnp.concatenate([far_rows[1], down], axis=0))
    high_rows = inner(from_above[halo : halo + 2 * migr], jnp.concatenate([up, far_rows[0]], axis=0))
    table[pl.ds(0, rows)] = moved
    table[pl.ds(rows, halo)] = from_below[0:halo] + low_rows[halo:].astype(BF16)
    table[pl.ds(rows + halo, halo)] = from_above[0:halo] + high_rows[0:halo].astype(BF16)
    neigh[...] = (0.5 * dot(table[...], w_recv[...])).astype(BF16)
    centre[...] = 0.5 * dot(moved, w_send[...])

    agg[...] = jnp.zeros_like(agg)
    span = CH * rows

    def front(c):
        here = pl.ds(c * span, span)
        pre = dot(oh[here, :], neigh[...]) + jnp.concatenate([centre[...]] * CH, axis=0)
        act, slope = silu_pair(pre)
        low = act.astype(BF16)
        hid[here, :] = low
        ds1[here, :] = slope
        part, slope = silu_pair(below(dot(beside(low), w_pair[...])) + mask[here, :])
        md[here, :] = slope
        total = part[0:rows]
        for u in range(1, CH):
            total = total + part[u * rows : (u + 1) * rows]
        agg[...] += total

    for c in range(slots // CH):
        front(c)

    if two_on:
        pl.semaphore_wait(two_sem, len(two_on))
    pass_on(four_sem, four_on)

    moved = table[pl.ds(0, rows)]
    agg_b = agg[...].astype(BF16)
    act, slope = silu_pair(0.5 * (dot(moved, w_self[...]) + dot(agg_b, w_agg[...])))
    node_hid = act.astype(BF16)
    updated_ref[...] = (moved.astype(F32) + dot(node_hid, w_out[...])).astype(BF16)
    d_node_pre = (0.5 * d_hid * slope).astype(BF16)
    d_agg[...] = 0.5 * by_transpose(d_node_pre, w_agg[...])
    g_out = inner(node_hid, cot[...])
    g_self = inner(moved, d_node_pre)
    g_agg = inner(agg_b, d_node_pre)
    if over_y:
        pl.semaphore_wait(y_sem, len(over_y))
    early = Sum(n_grp, n_y, n_z, 3, 2, False, reduce_scratch[:6])
    late = Sum(n_grp, n_y, n_z, 3, 1, True, reduce_scratch[6:])
    early.share([g_self, g_agg, g_out])
    d_local = cot[...].astype(F32) + by_transpose(d_node_pre, w_self[...])

    d_centre[...] = jnp.zeros_like(d_centre)
    d_neigh[...] = jnp.zeros_like(d_neigh)
    g_msg[...] = jnp.zeros_like(g_msg)

    def back(c):
        here = pl.ds(c * span, span)
        d_pre2 = (jnp.concatenate([d_agg[...]] * CH, axis=0) * md[here, :]).astype(BF16)
        d_pre = by_transpose(d_pre2, w_half[...]) * ds1[here, :]
        g_msg[...] += inner(hid[here, :], d_pre2)
        total = d_pre[0:rows]
        for u in range(1, CH):
            total = total + d_pre[u * rows : (u + 1) * rows]
        d_centre[...] += total
        low = d_pre.astype(BF16)
        first = low * left[here, :]
        sides = jnp.concatenate([first, low - first], axis=1)
        d_neigh[...] += dot(oht[c], sides)

    for c in range(slots // CH):
        back(c)

    d_neigh_b = below(d_neigh[...]).astype(BF16)
    d_centre_b = d_centre[...].astype(BF16)
    moved = table[pl.ds(0, rows)]
    g_recv = inner(table[...], d_neigh_b)
    g_send = inner(moved, d_centre_b)
    late.share([g_send, g_recv, g_msg[...]])
    ret_snd[...] = by_transpose(d_neigh_b[rows:], w_recv[...]).astype(BF16)
    returning = [
        send_to(ret_snd.at[pl.ds(0, halo)], ret_rcv.at[pl.ds(halo, halo)], 4, lower),
        send_to(ret_snd.at[pl.ds(halo, halo)], ret_rcv.at[pl.ds(0, halo)], 5, upper),
    ]
    for copy in returning:
        copy.start()
    if four_on:
        pl.semaphore_wait(four_sem, len(four_on))
    early.line()
    d_local = d_local + by_transpose(d_centre_b, w_send[...])
    d_local = d_local + by_transpose(d_neigh_b[0:rows], w_recv[...])
    for copy in returning:
        copy.wait()
    d_local = d_local + dot(send_hot, ret_rcv[...])
    grad_ref[...] = d_local.astype(BF16)
    late.line()
    early.spread()
    late.spread()
    early.finish(steps_ref, 3)
    late.finish(steps_ref, 0)


def shards(n_grp, n_y, n_z, *args):
    nodes, leave_list, arrive_list, send_list, neighbours, valid = args[:6]
    weights, cotangent = args[6:12], args[12]
    operands = (
        nodes[0],
        leave_list,
        arrive_list,
        send_list,
        neighbours[0].T,
        valid[0].T,
        *weights,
        cotangent[0],
    )
    operands = [pltpu.with_memory_space_constraint(x, pltpu.HBM) for x in operands]
    rows, width = operands[0].shape
    slots = operands[4].shape[0]
    migr, halo = leave_list.shape[1] // 2, send_list.shape[1] // 2
    table_rows = rows + 2 * halo
    edges = rows * slots
    plane = n_grp * n_y
    scratch = [pltpu.VMEM(x.shape, x.dtype) for x in operands]
    scratch += [
        pltpu.SemaphoreType.DMA((N_IN,)),
        pltpu.SemaphoreType.DMA((12,)),
        pltpu.SemaphoreType.REGULAR,
        pltpu.SemaphoreType.REGULAR,
        pltpu.SemaphoreType.REGULAR,
        pltpu.VMEM((2 * width, 2 * width), BF16),
        pltpu.VMEM((width, width), BF16),
        pltpu.VMEM((edges, width), BF16),
        pltpu.VMEM((2, halo + 3 * migr, width), BF16),
        pltpu.VMEM((2, halo + 3 * migr, width), BF16),
        pltpu.VMEM((2, migr, width), BF16),
        pltpu.VMEM((table_rows, width), BF16),
        pltpu.VMEM((2 * halo, width), BF16),
        pltpu.VMEM((2 * halo, width), BF16),
        pltpu.VMEM((slots, rows), jnp.int32),
        pltpu.VMEM((edges, table_rows), BF16),
        pltpu.VMEM((slots // CH, table_rows // 2, CH * rows), BF16),
        pltpu.VMEM((edges, width), F32),
        pltpu.VMEM((table_rows, width), BF16),
        pltpu.VMEM((rows, width), F32),
        pltpu.VMEM((rows, width), F32),
        pltpu.VMEM((edges, width), BF16),
        pltpu.VMEM((edges, width), F32),
        pltpu.VMEM((edges, width), F32),
        pltpu.VMEM((rows, width), F32),
        pltpu.VMEM((rows, width), F32),
        pltpu.VMEM((table_rows // 2, 2 * width), F32),
        pltpu.VMEM((width, width), F32),
    ]
    scratch += sum_scratch(plane, n_z, 3, 2) + sum_scratch(plane, n_z, 3, 1)
    both, weight_steps = pl.pallas_call(
        functools.partial(kernel, n_grp, n_y, n_z, (rows, slots, migr, halo)),
        out_shape=(
            jax.ShapeDtypeStruct((2, rows, width), BF16),
            jax.ShapeDtypeStruct((6, width, width), F32),
        ),
        in_specs=[pl.BlockSpec(memory_space=pltpu.HBM)] * N_IN,
        out_specs=[pl.BlockSpec(memory_space=pltpu.VMEM)] * 2,
        scratch_shapes=scratch,
        compiler_params=pltpu.CompilerParams(
            collective_id=0, has_side_effects=True, vmem_limit_bytes=52 * 1024 * 1024
        ),
        name="particle_step",
    )(*operands)
    return (both[0][None], both[1][None], weight_steps)


def solution(mesh):
    n_grp, n_slab = mesh.shape["grp"], mesh.shape["slab"]
    n_z = 16 if n_slab > 16 else n_slab // 2
    in_specs = (
        P("grp", "slab", None),
        P("grp", "slab"),
        P("grp", "slab"),
        P("grp", "slab"),
        P("grp", "slab", None),
        P("grp", "slab", None),
        P(),
        P(),
        P(),
        P(),
        P(),
        P(),
        P("grp", "slab", None),
    )
    out_specs = (P("grp", "slab", None), P("grp", "slab", None), P())
    return jax.shard_map(
        functools.partial(shards, n_grp, n_slab // n_z, n_z),
        mesh=mesh,
        in_specs=in_specs,
        out_specs=out_specs,
        check_vma=False,
    )
```

```python
import functools

import jax
import jax.numpy as jnp
from jax import lax
from jax.experimental import pallas as pl
from jax.experimental.pallas import tpu as pltpu
from jax.sharding import PartitionSpec as P

MESH = pl.DeviceIdType.MESH
F32 = jnp.float32
BF16 = jnp.bfloat16


def silu_pair(half):
    up = 1.0 + jnp.tanh(half)
    act = half * up
    return act, up + act * (2.0 - up)


def dot(left, right):
    return lax.dot_general(left, right, (((1,), (0,)), ((), ())), preferred_element_type=F32)


def inner(left, right):
    return lax.dot_general(left, right, (((0,), (0,)), ((), ())), preferred_element_type=F32)


def by_transpose(left, right):
    return lax.dot_general(left, right, (((1,), (1,)), ((), ())), preferred_element_type=F32)


def twice(weights):
    zero = jnp.zeros_like(weights)
    return jnp.concatenate(
        [
            jnp.concatenate([weights, zero], axis=1),
            jnp.concatenate([zero, weights], axis=1),
        ],
        axis=0,
    )


def beside(rows):
    middle = rows.shape[0] // 2
    return jnp.concatenate([rows[:middle], rows[middle:]], axis=1)


def below(rows):
    middle = rows.shape[1] // 2
    return jnp.concatenate([rows[:, :middle], rows[:, middle:]], axis=0)


def half(weights):
    return (0.5 * weights.astype(F32)).astype(BF16)


def hot(index, shape, dim):
    place = lax.broadcasted_iota(jnp.int32, shape, dim)
    return jnp.where(place == index, 1.0, 0.0).astype(BF16)


def bytes_of(ref, sem):
    return pltpu.make_async_copy(ref, ref, sem)


class Sum:
    def __init__(self, n_grp, n_y, n_z, mats, least, from_end, scratch):
        self.n_grp, self.n_y, self.n_z = n_grp, n_y, n_z
        self.mats = mats
        self.plane = n_grp * n_y
        self.per, self.owners = shares(self.plane, mats, least)
        self.offset = self.plane - self.owners if from_end else 0
        self.snd, self.rcv, self.part, self.zrcv, self.all, self.sems = scratch
        self.g = lax.axis_index("grp")
        slab = lax.axis_index("slab")
        self.y, self.z = slab // n_z, lax.rem(slab, n_z)
        self.q = self.g * n_y + self.y
        self.block = lax.rem(self.q + self.plane - self.offset, self.plane)
        self.is_owner = self.block < self.owners

    def device(self, q, z):
        return (q // self.n_y, lax.rem(q, self.n_y) * self.n_z + z)

    def copy(self, src, dst, phase, to):
        return pltpu.make_async_remote_copy(
            src_ref=src,
            dst_ref=dst,
            send_sem=self.sems.at[2 * phase],
            recv_sem=self.sems.at[2 * phase + 1],
            device_id=to,
            device_id_type=MESH,
        )

    def share(self, grads):
        tiles = 8
        for m in range(self.mats):
            low = grads[m].astype(BF16)
            for t in range(tiles):
                b = m * tiles + t
                self.snd[b // self.per, b % self.per] = low[t * 16 : (t + 1) * 16]

        for slot, (dg, dy) in enumerate(self.far_first()):
            to_g, to_y = lax.rem(self.g + dg, self.n_grp), lax.rem(self.y + dy, self.n_y)
            to = to_g * self.n_y + to_y
            block = lax.rem(to + self.plane - self.offset, self.plane)

            @pl.when(block < self.owners)
            def _():
                self.copy(
                    self.snd.at[block], self.rcv.at[slot], 0, (to_g, to_y * self.n_z + self.z)
                ).start()

    def far_first(self):
        def hops(step):
            chips = (step[0] + 1) // 2
            return min(chips, self.n_grp // 2 - chips) + min(step[1], self.n_y - step[1])

        places = [(dg, dy) for dg in range(self.n_grp) for dy in range(self.n_y) if dg or dy]
        return sorted(places, key=hops, reverse=True)

    def line(self):
        @pl.when(self.is_owner)
        def _():
            others = self.plane - 1
            bytes_of(self.rcv.at[pl.ds(0, others)], self.sems.at[1]).wait()
            total = self.snd[self.block].astype(F32)
            for i in range(others):
                total = total + self.rcv[i].astype(F32)
            self.part[0] = total.astype(BF16)
            self.zrcv[self.n_z - 1] = total.astype(BF16)
            for t in sorted(range(1, self.n_z), key=lambda t: -min(t, self.n_z - t)):
                to = lax.rem(self.z + t, self.n_z)
                self.copy(
                    self.part.at[0], self.zrcv.at[self.n_z - 1 - t], 1, self.device(self.q, to)
                ).start()

    def spread(self):
        @pl.when(self.is_owner)
        def _():
            bytes_of(self.zrcv.at[pl.ds(0, self.n_z - 1)], self.sems.at[3]).wait()
            total = jnp.zeros(self.part.shape[1:], F32)
            for i in range(self.n_z):
                total = total + self.zrcv[self.slot_of(i)].astype(F32)
            self.part[1] = total.astype(BF16)
            self.all[self.block] = total.astype(BF16)

            for dg, dy in self.far_first():
                to = (
                    lax.rem(self.g + dg, self.n_grp),
                    lax.rem(self.y + dy, self.n_y) * self.n_z + self.z,
                )
                self.copy(self.part.at[1], self.all.at[self.block], 2, to).start()

    def slot_of(self, i):
        return lax.rem(self.n_z - 1 - (self.z - i) + 2 * self.n_z, self.n_z)

    def finish(self, out, first):
        own = self.is_owner

        @pl.when(own)
        def _():
            bytes_of(self.snd.at[pl.ds(0, self.owners - 1)], self.sems.at[0]).wait()
            bytes_of(self.zrcv.at[pl.ds(0, self.n_z - 1)], self.sems.at[2]).wait()
            bytes_of(self.rcv.at[pl.ds(0, self.plane - 1)], self.sems.at[4]).wait()
            if self.owners > 1:
                bytes_of(self.all.at[pl.ds(0, self.owners - 1)], self.sems.at[5]).wait()

        @pl.when(jnp.logical_not(own))
        def _():
            bytes_of(self.snd.at[pl.ds(0, self.owners)], self.sems.at[0]).wait()
            bytes_of(self.all.at[pl.ds(0, self.owners)], self.sems.at[5]).wait()

        for m in range(self.mats):
            tiles = []
            for t in range(8):
                b = m * 8 + t
                tiles.append(self.all[b // self.per, b % self.per])
            total = jnp.concatenate(tiles, axis=0).astype(F32)
            square = jnp.sum(jnp.sum(total * total, axis=0, keepdims=True), axis=1, keepdims=True)
            out[first + m] = total / jnp.sqrt(square * (1.0 / (128 * 128)) + 1e-06)


def shares(plane, mats, least):
    blocks = mats * 8
    per = max(-(-blocks // plane), least)
    while blocks % per:
        per += 1
    return per, blocks // per


def sum_scratch(plane, n_z, mats, least):
    per, owners = shares(plane, mats, least)
    return [
        pltpu.VMEM((owners, per, 16, 128), BF16),
        pltpu.VMEM((plane, per, 16, 128), BF16),
        pltpu.VMEM((2, per, 16, 128), BF16),
        pltpu.VMEM((n_z, per, 16, 128), BF16),
        pltpu.VMEM((owners, per, 16, 128), BF16),
        pltpu.SemaphoreType.DMA((6,)),
    ]


NO_EDGE = -1e30
N_IN = 13
CH = 8


def kernel(n_grp, n_y, n_z, dims, *refs):
    rows, slots, migr, halo = dims
    table_rows = rows + 2 * halo
    ins = refs[:N_IN]
    both_ref, steps_ref = refs[N_IN : N_IN + 2]
    updated_ref, grad_ref = both_ref.at[0], both_ref.at[1]
    scratch = refs[N_IN + 2 :]
    held = scratch[:N_IN]
    (
        in_sems,
        halo_sems,
        y_sem,
        two_sem,
        four_sem,
        w_pair,
        w_half,
        table_t,
        left,
        snd,
        rcv,
        far_rows,
        table,
        ret_snd,
        ret_rcv,
        row,
        oh,
        oht,
        mask,
        neigh,
        centre,
        agg,
        hid,
        ds1,
        md,
        d_agg,
        d_centre,
        d_neigh,
        g_msg,
    ) = scratch[N_IN : N_IN + 29]
    reduce_scratch = scratch[N_IN + 29 :]
    (nodes, leave, arrive, send, nbr, valid, w_send, w_recv, w_msg, w_self, w_agg, w_out, cot) = held

    g, slab = lax.axis_index("grp"), lax.axis_index("slab")
    n_slab = n_y * n_z
    y, z = slab // n_z, lax.rem(slab, n_z)
    plane = n_grp * n_y
    q = g * n_y + y
    lower = (g, lax.rem(slab + n_slab - 1, n_slab))
    upper = (g, lax.rem(slab + 1, n_slab))
    lower2 = (g, lax.rem(slab + n_slab - 2, n_slab))
    upper2 = (g, lax.rem(slab + 2, n_slab))

    loads = [pltpu.make_async_copy(ins[i], held[i], in_sems.at[i]) for i in range(N_IN)]
    def along(dy, dz):
        return (g, lax.rem(y + dy, n_y) * n_z + lax.rem(z + dz, n_z))

    def steps(distances, size):
        return sorted({d % size for d in distances} - {0})

    near = [lower, upper, lower2, upper2]
    near += [(lax.rem(g + d, n_grp), slab) for d in range(1, n_grp)]
    near += [along(d, 0) for d in range(1, n_y)]
    near += [along(0, d) for d in steps((1, -1, 2, -2), n_z)]
    barrier = pltpu.get_barrier_semaphore()
    for i, to in enumerate(near):
        if i == 4:
            for load in loads[:4]:
                load.start()
        pl.semaphore_signal(barrier, inc=1, device_id=to, device_id_type=MESH)
    for load in loads[4:]:
        load.start()

    def pass_on(sem, targets):
        for to in targets:
            pl.semaphore_signal(sem, inc=1, device_id=to, device_id_type=MESH)

    over_y = [along(d, 0) for d in range(1, n_y)]
    two_on = [along(0, d) for d in steps((2, -2), n_z)]
    four_on = [along(0, d) for d in steps((4, -4), n_z)]

    def send_to(src, dst, k, to):
        return pltpu.make_async_remote_copy(
            src_ref=src,
            dst_ref=dst,
            send_sem=halo_sems.at[2 * k],
            recv_sem=halo_sems.at[2 * k + 1],
            device_id=to,
            device_id_type=MESH,
        )

    for i in range(4):
        loads[i].wait()
    mine = nodes[...]
    arrive_hot = hot(arrive[...], (rows + 2 * migr, rows), 0)
    send_hot = hot(send[...], (rows, 2 * halo), 0)
    moving = inner(hot(leave[...], (rows, 2 * migr), 0), mine).astype(BF16)
    chosen = dot(arrive_hot, send_hot).astype(BF16)
    lent = inner(chosen[0:rows], mine).astype(BF16)
    picks = chosen[rows:]
    down, up = moving[0:migr], moving[migr:]
    for k, (part, leaving) in enumerate(((lent[0:halo], down), (lent[halo:], up))):
        snd[k, 0:halo] = part
        snd[k, halo : halo + 2 * migr] = picks
        snd[k, halo + 2 * migr :] = leaving
    pl.semaphore_wait(barrier, len(near))
    fetching = []
    for k, (near, far) in enumerate(((lower, lower2), (upper, upper2))):
        fetching.append(
            send_to(snd.at[k, pl.ds(halo + 2 * migr, migr)], far_rows.at[k], 2 + k, far)
        )
        fetching.append(send_to(snd.at[k], rcv.at[k], k, near))
    for copy in fetching:
        copy.start()
    pass_on(y_sem, over_y)
    pass_on(two_sem, two_on)
    for i in range(4, N_IN):
        loads[i].wait()
    row[...] = jnp.where(valid[...] > 0, nbr[...], table_rows)
    across = row[...].T
    middle = table_rows // 2
    for k in range(slots):
        index = across[:, k : k + 1]
        here = pl.ds(k * rows, rows)
        oh[here, :] = hot(index, (rows, table_rows), 1)
        index = jnp.broadcast_to(index, (rows, 128))
        mask[here, :] = jnp.where(index < table_rows, 0.0, NO_EDGE).astype(F32)
        left[here, :] = jnp.where(index < middle, 1.0, 0.0).astype(BF16)
    for k in range(slots):
        index = row[k : k + 1, :]
        index = jnp.where(index >= middle, index - middle, index)
        oht[k // CH, :, k % CH * rows : (k % CH + 1) * rows] = hot(index, (middle, rows), 0)
    d_hid = by_transpose(cot[...], w_out[...])
    w_half[...] = half(w_msg[...])
    w_pair[...] = twice(w_half[...])
    kept = inner(arrive_hot[0:rows], mine)
    for copy in fetching:
        copy.wait()

    from_below, from_above = rcv.at[1], rcv.at[0]
    low_new, high_new = from_below[halo + 2 * migr :], from_above[halo + 2 * migr :]
    moved = kept + inner(arrive_hot[rows:], jnp.concatenate([low_new, high_new], axis=0))
    moved = moved.astype(BF16)
    low_rows = inner(from_below[halo : halo + 2 * migr], jnp.concatenate([far_rows[1], down], axis=0))
    high_rows = inner(from_above[halo : halo + 2 * migr], jnp.concatenate([up, far_rows[0]], axis=0))
    table[pl.ds(0, rows)] = moved
    table[pl.ds(rows, halo)] = from_below[0:halo] + low_rows[halo:].astype(BF16)
    table[pl.ds(rows + halo, halo)] = from_above[0:halo] + high_rows[0:halo].astype(BF16)
    neigh[...] = (0.5 * dot(table[...], w_recv[...])).astype(BF16)
    centre[...] = 0.5 * dot(moved, w_send[...])

    agg[...] = jnp.zeros_like(agg)
    span = CH * rows

    def front(c):
        if c == 0:
            table_t[...] = table[...].T
        here = pl.ds(c * span, span)
        pre = dot(oh[here, :], neigh[...]) + jnp.concatenate([centre[...]] * CH, axis=0)
        act, slope = silu_pair(pre)
        low = act.astype(BF16)
        hid[here, :] = low
        ds1[here, :] = slope
        part, slope = silu_pair(below(dot(beside(low), w_pair[...])) + mask[here, :])
        md[here, :] = slope
        total = part[0:rows]
        for u in range(1, CH):
            total = total + part[u * rows : (u + 1) * rows]
        agg[...] += total

    for c in range(slots // CH):
        front(c)

    if two_on:
        pl.semaphore_wait(two_sem, len(two_on))
    pass_on(four_sem, four_on)

    moved = table[pl.ds(0, rows)]
    agg_b = agg[...].astype(BF16)
    act, slope = silu_pair(0.5 * (dot(moved, w_self[...]) + dot(agg_b, w_agg[...])))
    node_hid = act.astype(BF16)
    updated_ref[...] = (moved.astype(F32) + dot(node_hid, w_out[...])).astype(BF16)
    d_node_pre = (0.5 * d_hid * slope).astype(BF16)
    d_agg[...] = 0.5 * by_transpose(d_node_pre, w_agg[...])
    g_out = inner(node_hid, cot[...])
    g_self = dot(table_t[:, 0:rows], d_node_pre)
    g_agg = inner(agg_b, d_node_pre)
    if over_y:
        pl.semaphore_wait(y_sem, len(over_y))
    early = Sum(n_grp, n_y, n_z, 3, 2, False, reduce_scratch[:6])
    late = Sum(n_grp, n_y, n_z, 3, 1, True, reduce_scratch[6:])
    early.share([g_self, g_agg, g_out])
    d_local = cot[...].astype(F32) + by_transpose(d_node_pre, w_self[...])

    d_centre[...] = jnp.zeros_like(d_centre)
    d_neigh[...] = jnp.zeros_like(d_neigh)
    g_msg[...] = jnp.zeros_like(g_msg)

    def back(c):
        here = pl.ds(c * span, span)
        d_pre2 = (jnp.concatenate([d_agg[...]] * CH, axis=0) * md[here, :]).astype(BF16)
        d_pre = by_transpose(d_pre2, w_half[...]) * ds1[here, :]
        g_msg[...] += inner(hid[here, :], d_pre2)
        total = d_pre[0:rows]
        for u in range(1, CH):
            total = total + d_pre[u * rows : (u + 1) * rows]
        d_centre[...] += total
        low = d_pre.astype(BF16)
        first = low * left[here, :]
        sides = jnp.concatenate([first, low - first], axis=1)
        d_neigh[...] += dot(oht[c], sides)

    for c in range(slots // CH):
        back(c)

    d_neigh_b = below(d_neigh[...]).astype(BF16)
    d_centre_b = d_centre[...].astype(BF16)
    g_recv = dot(table_t[...], d_neigh_b)
    g_send = dot(table_t[:, 0:rows], d_centre_b)
    late.share([g_send, g_recv, g_msg[...]])
    ret_snd[...] = by_transpose(d_neigh_b[rows:], w_recv[...]).astype(BF16)
    returning = [
        send_to(ret_snd.at[pl.ds(0, halo)], ret_rcv.at[pl.ds(halo, halo)], 4, lower),
        send_to(ret_snd.at[pl.ds(halo, halo)], ret_rcv.at[pl.ds(0, halo)], 5, upper),
    ]
    for copy in returning:
        copy.start()
    if four_on:
        pl.semaphore_wait(four_sem, len(four_on))
    early.line()
    d_local = d_local + by_transpose(d_centre_b, w_send[...])
    d_local = d_local + by_transpose(d_neigh_b[0:rows], w_recv[...])
    for copy in returning:
        copy.wait()
    d_local = d_local + dot(send_hot, ret_rcv[...])
    grad_ref[...] = d_local.astype(BF16)
    late.line()
    early.spread()
    late.spread()
    early.finish(steps_ref, 3)
    late.finish(steps_ref, 0)


def shards(n_grp, n_y, n_z, *args):
    nodes, leave_list, arrive_list, send_list, neighbours, valid = args[:6]
    weights, cotangent = args[6:12], args[12]
    operands = (
        nodes[0],
        leave_list,
        arrive_list,
        send_list,
        neighbours[0].T,
        valid[0].T,
        *weights,
        cotangent[0],
    )
    operands = [pltpu.with_memory_space_constraint(x, pltpu.HBM) for x in operands]
    rows, width = operands[0].shape
    slots = operands[4].shape[0]
    migr, halo = leave_list.shape[1] // 2, send_list.shape[1] // 2
    table_rows = rows + 2 * halo
    edges = rows * slots
    plane = n_grp * n_y
    scratch = [pltpu.VMEM(x.shape, x.dtype) for x in operands]
    scratch += [
        pltpu.SemaphoreType.DMA((N_IN,)),
        pltpu.SemaphoreType.DMA((12,)),
        pltpu.SemaphoreType.REGULAR,
        pltpu.SemaphoreType.REGULAR,
        pltpu.SemaphoreType.REGULAR,
        pltpu.VMEM((2 * width, 2 * width), BF16),
        pltpu.VMEM((width, width), BF16),
        pltpu.VMEM((width, table_rows), BF16),
        pltpu.VMEM((edges, width), BF16),
        pltpu.VMEM((2, halo + 3 * migr, width), BF16),
        pltpu.VMEM((2, halo + 3 * migr, width), BF16),
        pltpu.VMEM((2, migr, width), BF16),
        pltpu.VMEM((table_rows, width), BF16),
        pltpu.VMEM((2 * halo, width), BF16),
        pltpu.VMEM((2 * halo, width), BF16),
        pltpu.VMEM((slots, rows), jnp.int32),
        pltpu.VMEM((edges, table_rows), BF16),
        pltpu.VMEM((slots // CH, table_rows // 2, CH * rows), BF16),
        pltpu.VMEM((edges, width), F32),
        pltpu.VMEM((table_rows, width), BF16),
        pltpu.VMEM((rows, width), F32),
        pltpu.VMEM((rows, width), F32),
        pltpu.VMEM((edges, width), BF16),
        pltpu.VMEM((edges, width), F32),
        pltpu.VMEM((edges, width), F32),
        pltpu.VMEM((rows, width), F32),
        pltpu.VMEM((rows, width), F32),
        pltpu.VMEM((table_rows // 2, 2 * width), F32),
        pltpu.VMEM((width, width), F32),
    ]
    scratch += sum_scratch(plane, n_z, 3, 2) + sum_scratch(plane, n_z, 3, 1)
    both, weight_steps = pl.pallas_call(
        functools.partial(kernel, n_grp, n_y, n_z, (rows, slots, migr, halo)),
        out_shape=(
            jax.ShapeDtypeStruct((2, rows, width), BF16),
            jax.ShapeDtypeStruct((6, width, width), F32),
        ),
        in_specs=[pl.BlockSpec(memory_space=pltpu.HBM)] * N_IN,
        out_specs=[pl.BlockSpec(memory_space=pltpu.VMEM)] * 2,
        scratch_shapes=scratch,
        compiler_params=pltpu.CompilerParams(
            collective_id=0, has_side_effects=True, vmem_limit_bytes=52 * 1024 * 1024
        ),
        name="particle_step",
    )(*operands)
    return (both[0][None], both[1][None], weight_steps)


def solution(mesh):
    n_grp, n_slab = mesh.shape["grp"], mesh.shape["slab"]
    n_z = 16 if n_slab > 16 else n_slab // 2
    in_specs = (
        P("grp", "slab", None),
        P("grp", "slab"),
        P("grp", "slab"),
        P("grp", "slab"),
        P("grp", "slab", None),
        P("grp", "slab", None),
        P(),
        P(),
        P(),
        P(),
        P(),
        P(),
        P("grp", "slab", None),
    )
    out_specs = (P("grp", "slab", None), P("grp", "slab", None), P())
    return jax.shard_map(
        functools.partial(shards, n_grp, n_slab // n_z, n_z),
        mesh=mesh,
        in_specs=in_specs,
        out_specs=out_specs,
        check_vma=False,
    )
```
